32 devices in a mesh: member: 4 (over z), row: 8 (over y, x, core).
Axes of the slice: x: 2, y: 2, z: 4, core: 2. Of those that a mesh axis runs over, the one named last changes fastest.
Arguments:
- action: bfloat16 [2048, 1024], P('row'), may hold values from -6 to 6
- state_term: bfloat16 [8, 2048, 4096], P('member', 'row'), may hold values from -6 to 6
- target: float32 [2048], P('row'), may hold values from -6 to 6
- weight_a: bfloat16 [8, 1024, 4096], P('member', 'row'), may hold values from -0.21875 to 0.21875
- value_w: bfloat16 [8, 4096], P('member'), may hold values from -0.0234375 to 0.0234375
Outputs:
- weight_grad: bfloat16 [8, 1024, 4096], P('member', 'row')
- value_grad: float32 [8, 4096], P('member')
- state_grad: bfloat16 [8, 2048, 4096], P('member', 'row')
- diversity: float32 [2048], P('row')
The draws below stay inside these ranges and needn't reach their ends.
All inputs are finite; a program needn't handle non-finite values.
Results may differ from the reference program's by a relative error of at most 0.03.
Values may be sent and summed in bfloat16 or wider, within the bound.
No kernel may reach another device: no remote copies, remote signals or barrier semaphores. Data moves between devices by JAX's collectives and lax.ppermute only.
A program may use at most 128 MiB of HBM per device.

```python
import jax
import jax.numpy as jnp
from jax import lax

A = 1024
H = 4096
ROW_DEV = 256
MEMBERS = 8
ROWS = 2048
N_ROW = 8


def draw_weight_a(key, part):
    key = jax.random.fold_in(key, 11)
    common = jnp.clip(jax.random.normal(jax.random.fold_in(key, 1), (A, H), jnp.float32), -5.0, 5.0)
    own = jnp.clip(jax.random.normal(jax.random.fold_in(key, 2), (MEMBERS, A, H), jnp.float32), -5.0, 5.0)
    mixed = 0.8 * common[None] + 0.6 * own
    return (mixed / jnp.sqrt(jnp.float32(A))).astype(jnp.bfloat16)


def steps_of(stream_key, shape, cuts, low, high):
    level, own = 1.0, jax.random.fold_in(stream_key, 6)
    for dim, shards_of in cuts:
        heights = jnp.exp(jax.random.uniform(jax.random.fold_in(own, dim), (shards_of,), jnp.float32, low / len(cuts), high / len(cuts)))
        level = level * jnp.repeat(heights, shape[dim] // shards_of).reshape([-1 if axis == dim else 1 for axis in range(len(shape))])
    return level


def centred(stream_key, dims, scale, limit, split=(), held_as=jnp.bfloat16):
    factor_of = steps_of(stream_key, dims, split, -0.22, 0.18) if split else 1.0
    drawn = jax.random.normal(stream_key, dims, jnp.float32) * scale * factor_of
    return jnp.minimum(jnp.maximum(drawn, -limit), limit).astype(held_as)


def setup_inputs(seed: int = 0) -> dict:
    key_of = jax.random.split(jax.random.key(seed), 6)
    action = centred(key_of[0], (ROWS, A), 1.0, 6.0, ((0, 8),))
    state_term = centred(key_of[1], (MEMBERS, ROWS, H), 1.0, 6.0, ((0, 4), (1, 8)))
    target = centred(key_of[2], (ROWS,), 1.0, 6.0, ((0, 8),), jnp.float32)
    weight_a = draw_weight_a(jax.random.fold_in(key_of[5], 71), 0)
    value_w = centred(key_of[4], (MEMBERS, H), (16 * H) ** -0.5, 0.0234375, ((0, 4),))
    return dict(action=action, state_term=state_term, target=target, weight_a=weight_a, value_w=value_w)


EPS = 1e-06
ETA = 5.0

def forward_member(weights, value_row, state_rows, action):
    pre_act = state_rows.astype(jnp.float32) + jnp.dot(action, weights, preferred_element_type=jnp.float32)
    sigmoid_part = jax.nn.sigmoid(pre_act)
    hidden = pre_act * sigmoid_part
    slope_first = sigmoid_part * (1.0 + pre_act * (1.0 - sigmoid_part))
    slope_second = sigmoid_part * (1.0 - sigmoid_part) * (2.0 + pre_act * (1.0 - 2.0 * sigmoid_part))
    value_float = value_row.astype(jnp.float32)
    q_value = lax.optimization_barrier(jnp.sum(hidden * value_float, axis=-1))
    tangent = (slope_first * value_float).astype(jnp.bfloat16)
    action_grad = lax.dot_general(tangent, weights, (((1,), (1,)), ((), ())), preferred_element_type=jnp.float32)
    grad_norm = jnp.sqrt(lax.optimization_barrier(jnp.sum(action_grad * action_grad, axis=-1, keepdims=True)) + EPS)
    unit_grad = action_grad / grad_norm
    return (hidden, slope_first, slope_second, q_value, tangent, unit_grad, grad_norm)

def reference(action, state_term, target, weight_a, value_w):

    def front(operands):
        weights, value_row, state_rows = operands
        outs_front = forward_member(weights, value_row, state_rows, action)
        return outs_front[5].astype(jnp.bfloat16)
    units = lax.map(front, (weight_a, value_w, state_term))
    unit_float = units.astype(jnp.float32)
    total = lax.optimization_barrier(jnp.sum(unit_float, axis=0))
    cross_sum = lax.optimization_barrier(jnp.sum(lax.optimization_barrier(jnp.sum(unit_float * total[None], axis=2)), axis=0))
    square_sum = lax.optimization_barrier(jnp.sum(lax.optimization_barrier(jnp.sum(unit_float * unit_float, axis=2)), axis=0))
    pairs = MEMBERS * (MEMBERS - 1)
    diversity = (cross_sum - square_sum) / pairs

    def back(operands):
        weights, value_row, state_rows, unit_b = operands
        hidden, slope_first, slope_second, q_value, tangent, unit_grad, grad_norm = forward_member(weights, value_row, state_rows, action)
        dir_grad = 2.0 * ETA / pairs * (total - unit_b.astype(jnp.float32))
        along = lax.optimization_barrier(jnp.sum(unit_grad * dir_grad, axis=-1, keepdims=True))
        cotangent = ((dir_grad - unit_grad * along) / grad_norm).astype(jnp.bfloat16)
        back_term = jnp.dot(cotangent, weights, preferred_element_type=jnp.float32)
        residue = (q_value - target)[:, None]
        value_float = value_row.astype(jnp.float32)
        pre_grad = value_float * (slope_first * residue + slope_second * back_term)
        value_grad = lax.optimization_barrier(jnp.sum(hidden * residue + slope_first * back_term, axis=0))
        pre_b = pre_grad.astype(jnp.bfloat16)
        left = jnp.concatenate([action.reshape(N_ROW, ROW_DEV, A), cotangent.reshape(N_ROW, ROW_DEV, A)], axis=1)
        right = jnp.concatenate([pre_b.reshape(N_ROW, ROW_DEV, H), tangent.reshape(N_ROW, ROW_DEV, H)], axis=1)

        def block_sum(accum, pieces):
            left_blk, right_blk = pieces
            partial_sum = lax.dot_general(left_blk, right_blk, (((0,), (0,)), ((), ())), preferred_element_type=jnp.float32)
            rounded = lax.optimization_barrier(partial_sum.astype(jnp.bfloat16))
            return (accum + rounded.astype(jnp.float32), None)
        grad_sum, unused = lax.scan(block_sum, jnp.zeros((A, H), jnp.float32), (left, right))
        return (grad_sum.astype(jnp.bfloat16), value_grad, pre_b)
    weight_grad, value_grad, state_grad = lax.map(back, (weight_a, value_w, state_term, units))
    return (weight_grad, value_grad, state_grad, diversity)
```

```python
import functools

import jax
import jax.numpy as jnp
from jax import lax
from jax.experimental import pallas as pl
from jax.experimental.pallas import tpu as pltpu
from jax.sharding import PartitionSpec as P

EPS = 1e-06
ETA = 5.0
UNIT = 512
GATHER_CUTS = ((4, 4), (4, 2, 2))
SCATTER_CUTS = ((1, 1, 2, 4), (4, 2, 2))
TILE = 512
STRIP = 16
F32 = jnp.float32
BF16 = jnp.bfloat16
PARAMS = dict(vmem_limit_bytes=16 * 1024 * 1024)
LIGHT = pl.CostEstimate(flops=1000000, bytes_accessed=100000, transcendentals=0)


def tie(x, *earlier):
    return lax.optimization_barrier((x,) + earlier)[0]


def in_hbm(xs):
    return [pltpu.with_memory_space_constraint(x, pltpu.HBM) for x in xs]


def plan(cuts, held, width):
    out = []
    for m in range(held):
        lo = 0
        for units in cuts[0] if m < held - 1 else cuts[1]:
            out.append((m, lo, units * UNIT))
            lo += units * UNIT
        assert lo == width
    return out


class Ring:
    def __init__(self, n_row):
        self.n_row = n_row
        self.chips = n_row // 2
        self.half = self.chips // 2
        order = list(range(self.half)) + [self.chips + self.half - 1 - p for p in range(self.half, self.chips)]
        up, down, swap = [], [], []
        for pos in range(self.chips):
            for core in range(2):
                here = order[pos] * 2 + core
                step = 1 - 2 * core
                up.append((here, order[(pos + step) % self.chips] * 2 + core))
                down.append((here, order[(pos - step) % self.chips] * 2 + core))
                swap.append((here, order[pos] * 2 + 1 - core))
        self.up, self.down, self.swap = up, down, swap

    def onward(self, x):
        return lax.ppermute(x, "row", self.up)

    def backward(self, x):
        return lax.ppermute(x, "row", self.down)

    def partner(self, x):
        return lax.ppermute(x, "row", self.swap)

    def blocks(self):
        me = lax.axis_index("row")
        chip, core = me // 2, me % 2
        flip = self.chips + self.half - 1
        pos = jnp.where(chip < self.half, chip, flip - chip)

        def index(p, c):
            p = (p + 2 * self.chips) % self.chips
            return jnp.where(p < self.half, p, flip - p) * 2 + c

        out = []
        for c, step in ((core, 1 - 2 * core), (1 - core, 2 * core - 1)):
            out.append(index(pos, c))
            for t in range(1, self.half):
                out.append(index(pos - step * t, c))
                out.append(index(pos - step * t, 1 - c))
            out.append(index(pos - step * self.half, c))
        return jnp.stack(out).astype(jnp.int32)


def slopes(pre):
    turn = jnp.tanh(0.5 * pre)
    sig = 0.5 * turn + 0.5
    rest = 1.0 - sig
    spread = sig * rest
    one = sig + pre * spread
    two = spread * (2.0 - pre * turn)
    return pre * sig, one, two


def inverse_norm(g):
    return 1.0 / jnp.sqrt(jnp.sum(g * g, axis=-1, keepdims=True) + EPS)


def full(shape):
    return pl.BlockSpec(shape, lambda *_: (0,) * len(shape))


def permute_action(action, blocks):
    rows, width = action.shape
    count = blocks.shape[0]
    size = width // count
    if size % 128:
        moved = jnp.take(action.reshape(rows, count, size), blocks, axis=1).reshape(rows, width)
        return moved, moved.T

    def kernel(idx_ref, x_ref, out_ref, turned_ref):
        x = x_ref[...]
        out_ref[...] = x
        turned_ref[...] = x.astype(F32).T.astype(BF16)

    return pl.pallas_call(
        kernel,
        grid_spec=pltpu.PrefetchScalarGridSpec(
            num_scalar_prefetch=1,
            grid=(count,),
            in_specs=[pl.BlockSpec((rows, size), lambda j, idx: (0, idx[j]))],
            out_specs=[
                pl.BlockSpec((rows, size), lambda j, idx: (0, j)),
                pl.BlockSpec((size, rows), lambda j, idx: (j, 0)),
            ],
        ),
        out_shape=[
            jax.ShapeDtypeStruct((rows, width), BF16),
            jax.ShapeDtypeStruct((width, rows), BF16),
        ],
        compiler_params=pltpu.CompilerParams(**PARAMS),
        cost_estimate=LIGHT,
        name="permute_action",
    )(blocks, action)


def front(member, lo, action, state, weight_a, pieces, value_w, carry):
    rows, width = action.shape
    size, cols = pieces[0].shape
    tile = min(TILE, cols)
    steps = cols // tile
    base = lo // tile
    held = weight_a.shape[0]
    n_in = 4 + len(pieces)

    def kernel(*refs):
        action_ref, state_ref, own_ref, value_ref = refs[:4]
        rest = refs[4:n_in]
        pre_ref, q_ref, g_ref = refs[-3:]

        @pl.when(pl.program_id(0) == 0)
        def _():
            if carry is None:
                q_ref[...] = jnp.zeros_like(q_ref)
                g_ref[...] = jnp.zeros_like(g_ref)
            else:
                q_ref[...] = refs[n_in][...]
                g_ref[...] = refs[n_in + 1][...]

        weights = jnp.concatenate([own_ref[0]] + [r[...] for r in rest], axis=0)
        pre_ref[...] = jnp.dot(action_ref[...], weights, preferred_element_type=F32)
        value = value_ref[pl.ds(member, 1), :].astype(F32)
        tangents = []
        for r in range(0, rows, STRIP):
            cut = pl.ds(r, STRIP)
            pre = pre_ref[cut, :] + state_ref[0, cut, :].astype(F32)
            pre_ref[cut, :] = pre
            hidden, one, _ = slopes(pre)
            prod = hidden * value
            lanes = prod[:, :128]
            for c in range(128, tile, 128):
                lanes = lanes + prod[:, c : c + 128]
            q_ref[cut, :] += lanes
            tangents.append((one * value).astype(BF16))
        tangent = jnp.concatenate(tangents, axis=0)
        g_ref[...] += lax.dot_general(
            tangent, weights, (((1,), (1,)), ((), ())), preferred_element_type=F32
        )

    piece = pl.BlockSpec((size, tile), lambda j: (0, j))
    in_specs = [
        full((rows, width)),
        pl.BlockSpec((1, rows, tile), lambda j: (member, 0, base + j)),
        pl.BlockSpec((1, size, tile), lambda j: (member, 0, base + j)),
        pl.BlockSpec((held, tile), lambda j: (0, base + j)),
    ] + [piece] * len(pieces)
    args = [action, state, weight_a, value_w] + list(pieces)
    aliases = {}
    if carry is not None:
        in_specs += [full((rows, 128)), full((rows, width))]
        args += list(carry)
        aliases = {n_in: 1, n_in + 1: 2}
    return pl.pallas_call(
        kernel,
        grid=(steps,),
        in_specs=in_specs,
        out_specs=[pl.BlockSpec((rows, tile), lambda j: (0, j)), full((rows, 128)), full((rows, width))],
        out_shape=[
            pltpu.HBM((rows, cols), F32),
            pltpu.HBM((rows, 128), F32),
            pltpu.HBM((rows, width), F32),
        ],
        input_output_aliases=aliases,
        compiler_params=pltpu.CompilerParams(**PARAMS),
        cost_estimate=LIGHT,
        name="front",
    )(*in_hbm(args[:4]), *args[4:])


def unit_sums(bit, grads):
    rows, width = grads[0].shape
    half = rows // 2
    part = half // 2
    count = len(grads)

    def kernel(bit_ref, *refs):
        keeps, sends, square_ref = refs[count : count + 2], refs[count + 2 : count + 4], refs[count + 4]
        total = jnp.zeros((half, width), F32)
        square = jnp.zeros((half, 1), F32)
        for g_ref in refs[:count]:
            g = g_ref[...]
            unit = (g * inverse_norm(g)).astype(BF16).astype(F32)
            total = total + unit
            square = square + jnp.sum(unit * unit, axis=-1, keepdims=True)
        square_ref[...] = square
        step = pl.program_id(0)

        @pl.when(step == 0)
        def _():
            for i, ref in enumerate(sends):
                ref[...] = total[i * part : (i + 1) * part].astype(BF16)

        @pl.when(step == 1)
        def _():
            for i, ref in enumerate(keeps):
                ref[...] = total[i * part : (i + 1) * part]

    def place(j, bit):
        return (1 - j + bit[0] * (2 * j - 1), 0)

    def fixed(j, bit):
        return (0, 0)

    return pl.pallas_call(
        kernel,
        grid_spec=pltpu.PrefetchScalarGridSpec(
            num_scalar_prefetch=1,
            grid=(2,),
            in_specs=[pl.BlockSpec((half, width), place)] * count,
            out_specs=[pl.BlockSpec((part, width), fixed)] * 4 + [pl.BlockSpec((half, 1), place)],
        ),
        out_shape=[jax.ShapeDtypeStruct((part, width), F32)] * 2
        + [jax.ShapeDtypeStruct((part, width), BF16)] * 2
        + [jax.ShapeDtypeStruct((rows, 1), F32)],
        compiler_params=pltpu.CompilerParams(**PARAMS),
        cost_estimate=LIGHT,
        name="unit_sums",
    )(bit, *in_hbm(grads))


def cotangent(bit, scale, n_member, kept, sent, got, turned_action, q, target, g):
    rows, width = g.shape
    half = rows // 2
    part = half // 2

    def kernel(bit_ref, *refs):
        kept_refs, sent_refs, got_refs, turned_action_ref = refs[:2], refs[2:4], refs[4:6], refs[6]
        q_ref, target_ref, g_ref, cot_ref, left_ref, resid_ref, length_ref, total_ref = refs[7:]
        resid_ref[...] = jnp.sum(q_ref[...], axis=-1, keepdims=True) - target_ref[...]
        step = pl.program_id(0)

        @pl.when(step == 0)
        def _():
            for i in range(2):
                total_ref[pl.ds(i * part, part), :] = kept_refs[i][...]
            left_ref[:, pl.ds(0, rows)] = turned_action_ref[...]

        @pl.when(step == 1)
        def _():
            for i in range(2):
                total_ref[pl.ds(i * part, part), :] = (
                    n_member * sent_refs[i][...].astype(F32) + got_refs[i][...].astype(F32)
                )

        total = total_ref[...]
        grad = g_ref[...]
        inverse = inverse_norm(grad)
        unit = grad * inverse
        direction = scale * (total - unit.astype(BF16).astype(F32))
        along = jnp.sum(unit * direction, axis=-1, keepdims=True)
        cot = (direction - unit * along) * inverse
        cot_ref[...] = cot.astype(BF16)
        turned = cot.T.astype(BF16)
        for place in range(2):

            @pl.when((step + bit_ref[0]) % 2 == place)
            def _():
                left_ref[:, pl.ds(rows + place * half, half)] = turned

        length_ref[...] = jnp.sum(total * total, axis=-1, keepdims=True)

    def place(j, bit):
        return (j + bit[0] * (1 - 2 * j), 0)

    def fixed(j, bit):
        return (0, 0)

    return pl.pallas_call(
        kernel,
        grid_spec=pltpu.PrefetchScalarGridSpec(
            num_scalar_prefetch=1,
            grid=(2,),
            in_specs=[pl.BlockSpec((part, width), fixed)] * 6
            + [
                pl.BlockSpec((width, rows), fixed),
                pl.BlockSpec((half, 128), place),
                pl.BlockSpec((half, 1), place),
                pl.BlockSpec((half, width), place),
            ],
            out_specs=[
                pl.BlockSpec((half, width), place),
                pl.BlockSpec((width, 2 * rows), fixed),
                pl.BlockSpec((half, 1), place),
                pl.BlockSpec((half, 1), place),
            ],
            scratch_shapes=[pltpu.VMEM((half, width), F32)],
        ),
        out_shape=[
            pltpu.HBM((rows, width), BF16),
            pltpu.HBM((width, 2 * rows), BF16),
            pltpu.HBM((rows, 1), F32),
            jax.ShapeDtypeStruct((rows, 1), F32),
        ],
        compiler_params=pltpu.CompilerParams(**PARAMS),
        cost_estimate=LIGHT,
        name="cotangent",
    )(bit, *kept, *sent, *got, *in_hbm([turned_action, q, target, g]))


def back(member, lo, cols, offset, cot, left, weight_a, pieces, value_w, pre, resid, grads, shape):
    rows, width = cot.shape
    size = pieces[0].shape[0]
    tile = min(TILE, cols)
    steps = cols // tile
    base, inner = lo // tile, offset // tile
    held = weight_a.shape[0]
    n_in = 6 + len(pieces)
    mid = width // 2
    part = min(256, tile)

    def kernel(*refs):
        cot_ref, left_ref, own_ref, value_ref, pre_ref, resid_ref = refs[:6]
        rest = refs[6:n_in]
        state_ref, sums_ref, top_ref, bottom_ref = refs[-5:-1]
        back_ref = refs[-1]
        starts = range(0, tile, part)
        for c in starts:
            lanes = pl.ds(c, part)
            weights = jnp.concatenate([own_ref[0, :, lanes]] + [r[:, lanes] for r in rest], axis=0)
            back_ref[:, lanes] = jnp.dot(cot_ref[...], weights, preferred_element_type=F32)
        for c in starts:
            lanes = pl.ds(c, part)
            value = value_ref[pl.ds(member, 1), lanes].astype(F32)
            sums = jnp.zeros((8, part), F32)
            dpres, tangents = [], []
            for r in range(0, rows, STRIP):
                cut = pl.ds(r, STRIP)
                hidden, one, two = slopes(pre_ref[cut, lanes])
                back_term = back_ref[cut, lanes]
                resid_here = resid_ref[cut, :]
                dpre = (value * (one * resid_here + two * back_term)).astype(BF16)
                state_ref[0, cut, lanes] = dpre
                term = hidden * resid_here + one * back_term
                for s in range(0, STRIP, 8):
                    sums = sums + term[s : s + 8]
                dpres.append(dpre)
                tangents.append((one * value).astype(BF16))
            sums_ref[0, :, lanes] = jnp.sum(sums, axis=0, keepdims=True)
            right = jnp.concatenate(dpres + tangents, axis=0)
            bottom_ref[:, lanes] = jnp.dot(
                left_ref[pl.ds(mid, mid), :], right, preferred_element_type=F32
            ).astype(BF16)
            top_ref[:, lanes] = jnp.dot(
                left_ref[pl.ds(0, mid), :], right, preferred_element_type=F32
            ).astype(BF16)

    piece = pl.BlockSpec((size, tile), lambda j: (0, inner + j))
    in_specs = [
        full((rows, width)),
        full((width, 2 * rows)),
        pl.BlockSpec((1, size, tile), lambda j: (member, 0, base + j)),
        pl.BlockSpec((held, tile), lambda j: (0, base + j)),
        pl.BlockSpec((rows, tile), lambda j: (0, inner + j)),
        full((rows, 1)),
    ] + [piece] * len(pieces)
    args = [cot, left, weight_a, value_w, pre, resid] + list(pieces)
    aliases = {}
    if grads is not None:
        in_specs += [pl.BlockSpec(memory_space=pl.ANY)] * 2
        args += list(grads)
        aliases = {n_in: 0, n_in + 1: 1}
    return pl.pallas_call(
        kernel,
        grid=(steps,),
        in_specs=in_specs,
        out_specs=[
            pl.BlockSpec((1, rows, tile), lambda j: (member, 0, base + j)),
            pl.BlockSpec((1, 1, tile), lambda j: (member, 0, base + j)),
            pl.BlockSpec((mid, tile), lambda j: (0, j)),
            pl.BlockSpec((mid, tile), lambda j: (0, j)),
        ],
        out_shape=[
            pltpu.HBM(shape, BF16),
            pltpu.HBM((held, 1, shape[-1]), F32),
            pltpu.HBM((mid, cols), BF16),
            jax.ShapeDtypeStruct((mid, cols), BF16),
        ],
        scratch_shapes=[pltpu.VMEM((rows, tile), F32)],
        input_output_aliases=aliases,
        compiler_params=pltpu.CompilerParams(**PARAMS),
        cost_estimate=LIGHT,
        name="back",
    )(*in_hbm(args[:6]), *args[6:])


def combine(size, jobs, final, weight_grad, shape):
    in_specs, args = [], []
    out_specs, out_shape = [], []

    def take(addends):
        cols = addends[0][0].shape[1]
        for i, (array, block) in enumerate(addends):
            array = array if i else in_hbm([array])[0]
            in_specs.append(pl.BlockSpec((size, cols), functools.partial(lambda b, *_: (b, 0), block)))
            args.append(array)
        return len(addends)

    counts = [[take(addends) for addends in job] for job in jobs]
    for job in jobs:
        cols = job[0][0][0].shape[1]
        out_specs.append(full((len(job) * size, cols)))
        out_shape.append(jax.ShapeDtypeStruct((len(job) * size, cols), BF16))
    if final is not None:
        member, lo, addends = final
        cols = addends[0][0].shape[1]
        counts.append([take(addends)])
        out_specs.append(pl.BlockSpec((1, size, cols), lambda *_: (member, 0, lo // cols)))
        out_shape.append(pltpu.HBM(shape, BF16))
    n_in = len(args)
    aliases = {}
    if final is not None and weight_grad is not None:
        in_specs.append(pl.BlockSpec(memory_space=pl.ANY))
        args.append(weight_grad)
        aliases = {n_in: len(jobs)}

    def kernel(*refs):
        outs = refs[len(args) :]
        at = 0
        for i, parts in enumerate(counts):
            for p, count in enumerate(parts):
                addends = refs[at : at + count]
                at += count
                for r in range(0, size, STRIP):
                    total = addends[0][pl.ds(r, STRIP), :].astype(F32)
                    for ref in addends[1:]:
                        total = total + ref[pl.ds(r, STRIP), :].astype(F32)
                    if i < len(jobs):
                        outs[i][pl.ds(p * size + r, STRIP), :] = total.astype(BF16)
                    else:
                        outs[i][0, pl.ds(r, STRIP), :] = total.astype(BF16)

    outs = pl.pallas_call(
        kernel,
        grid=(1,),
        in_specs=in_specs,
        out_specs=out_specs,
        out_shape=out_shape,
        input_output_aliases=aliases,
        compiler_params=pltpu.CompilerParams(**PARAMS),
        cost_estimate=LIGHT,
        name="combine",
    )(*args)
    return outs[: len(jobs)], (outs[-1] if final is not None else weight_grad)


def butterfly(x, axis, size, start=1):
    bit = start
    while bit < size:
        x = x + lax.ppermute(x, axis, [(i, i ^ bit) for i in range(size)])
        bit *= 2
    return x


def member_total(kept, sent, size):
    pair = [(i, i ^ 1) for i in range(size)]
    firsts = [lax.ppermute(x, "member", pair).astype(F32) for x in sent]
    totals = [a + b for a, b in zip(kept, firsts)]
    bit = 2
    while bit < size:
        swap = [(i, i ^ bit) for i in range(size)]
        totals = [x + lax.ppermute(x.astype(BF16), "member", swap).astype(F32) for x in totals]
        bit *= 2
    got = [lax.ppermute((x - size * first).astype(BF16), "member", pair) for x, first in zip(totals, firsts)]
    return totals, got


def body(n_member, n_row, action, state_term, target, weight_a, value_w):
    ring = Ring(n_row)
    chips, half = ring.chips, ring.half
    held, size, hidden_width = weight_a.shape
    members = held * n_member
    pairs = members * (members - 1)
    rows = action.shape[0]
    member_index = lax.axis_index("member")
    bit = (member_index % 2).astype(jnp.int32).reshape(1)
    action_here, turned_action = permute_action(action, ring.blocks())

    chunks = plan(GATHER_CUTS, held, hidden_width)
    count = len(chunks)
    pieces, pres, carry = {}, {}, [None] * held
    links, chains, swaps = [], {}, {}

    def send(x, *earlier):
        links.append(ring.onward(tie(x, *links[-2:-1], *earlier)))
        return links[-1]

    def run_front(c):
        m, lo, _ = chunks[c]
        pres[m, lo], *carry[m] = front(m, lo, action_here, state_term, weight_a, pieces[m, lo], value_w, carry[m])
        return carry[m][0]

    def open_chunk(c, *earlier):
        m, lo, cols = chunks[c]
        own = weight_a[m, :, lo : lo + cols]
        first = ring.partner(own)
        mine, a, b = [], own, first
        for _ in range(1, half):
            a = send(a, *earlier)
            b = send(b)
            mine += [a, b]
        chains[c] = (a, mine, first)
        swaps[c] = [ring.partner(x) for x in mine]

    def close_chunk(c):
        m, lo, _ = chunks[c]
        a, mine, first = chains[c]
        last = send(a)
        pieces[m, lo] = mine + [last, first] + swaps[c] + [ring.partner(last)]

    open_chunk(0)
    for c in range(1, count):
        open_chunk(c, *([run_front(c - 3)] if c >= 3 else []))
        close_chunk(c - 1)
    close_chunk(count - 1)
    for c in range(max(count - 3, 0), count):
        run_front(c)
    gs = [c[1] for c in carry]

    *kept_sent, square = unit_sums(bit, gs)
    kept, sent = kept_sent[:2], kept_sent[2:]
    totals, got = member_total(kept, sent, n_member)
    cots = [
        cotangent(bit, 2.0 * ETA / pairs, n_member, totals, sent, got, turned_action, q, target[:, None], g)
        for q, g in carry
    ]
    counted = ((jnp.arange(rows) // (rows // 2)) == bit[0]) & (member_index < 2)
    lengths = jnp.where(counted, cots[0][3][:, 0], 0.0) - square[:, 0]
    diversity = butterfly(lengths, "member", n_member) / pairs

    chunks = plan(SCATTER_CUTS, held, hidden_width)
    count = len(chunks)
    grads = weight_grad = None
    tops, others, flows, swapped = {}, {}, {}, {}
    queue = []

    def run_back(c, *earlier):
        nonlocal grads
        m, lo, cols = chunks[c]
        start = max(l for mm, l in pieces if mm == m and l <= lo)
        pre = tie(pres[m, start], *earlier) if earlier else pres[m, start]
        cot, left, resid, _ = cots[m]
        *grads, tops[c], bottom = back(
            m, lo, cols, lo - start, cot, left, weight_a, pieces[m, start],
            value_w, pre, resid, grads, state_term.shape,
        )
        others[c] = ring.partner(bottom)
        return bottom

    def addends(c, place, *more):
        return [(tops[c], place), (others[c], place), *more]

    lead = 2
    for c in range(lead):
        run_back(c)
    finish_at = {}
    for c in range(count):
        finish_at.setdefault(min(c + half + 1, count - 1 + half), []).append(c)
    after = None
    for s in range(count + half):
        jobs, labels = [], []
        for t in range(half):
            c = s - t
            if not 0 <= c < count:
                continue
            job = [addends(c, 2 * (half - t) - 1, *([(flows[c], 0)] if t else []))]
            if t:
                job.append(addends(c, 2 * (half - t), *([(flows[c], 1)] if t > 1 else [])))
            jobs.append(job)
            labels.append((c, t))
        if after is not None and jobs:
            tops[s] = tie(tops[s], after)
            jobs[0] = [addends(s, 2 * half - 1)]
        finals = [
            (chunks[c][0], chunks[c][1], addends(c, 0, (flows[c], 0), (swapped[c], 1)))
            for c in finish_at.get(s, [])
        ]
        for final in finals[:-1]:
            _, weight_grad = combine(size, [], final, weight_grad, weight_a.shape)
        outs, weight_grad = combine(size, jobs, finals[-1] if finals else None, weight_grad, weight_a.shape)
        after = None
        if s + lead < count:
            after = run_back(s + lead, outs[0])
        for (c, t), x in zip(labels, outs):
            flows[c] = ring.backward(tie(x, *queue[-2:-1]))
            queue.append(flows[c])
            if t == half - 1:
                swapped[c] = ring.partner(flows[c])
    value_grad = butterfly(grads[1][:, 0, :], "row", n_row)
    state_grad = grads[0]
    return weight_grad, value_grad, state_grad, diversity


def solution(mesh):
    in_specs = (
        P("row", None),
        P("member", "row", None),
        P("row"),
        P("member", "row", None),
        P("member", None),
    )
    out_specs = (P("member", "row", None), P("member", None), P("member", "row", None), P("row"))
    step = functools.partial(body, mesh.shape["member"], mesh.shape["row"])
    return jax.shard_map(step, mesh=mesh, in_specs=in_specs, out_specs=out_specs, check_vma=False)
```

```python
import functools

import jax
import jax.numpy as jnp
from jax import lax
from jax.experimental import pallas as pl
from jax.experimental.pallas import tpu as pltpu
from jax.sharding import PartitionSpec as P

EPS = 1e-06
ETA = 5.0
UNIT = 512
GATHER_CUTS = ((2, 2, 2, 2), (2, 2, 2, 1, 1))
SCATTER_CUTS = ((1, 1, 2, 2, 2), (2, 2, 2, 1, 1))
LANES = 512
STRIP = 16
F32 = jnp.float32
BF16 = jnp.bfloat16
FLOPS_PER_US = 1153500000


def tie(x, *earlier):
    return lax.optimization_barrier((x,) + earlier)[0]


def in_vmem(xs):
    return [pltpu.with_memory_space_constraint(x, pltpu.VMEM) for x in xs]


def resident(kernel, name, ins, outs, scalars=(), scratch=(), hbm=(), aliases=None, micros=0.7):
    spaces = [pltpu.SMEM] * len(scalars) + [pltpu.VMEM] * len(ins) + [pl.ANY] * len(hbm)
    return pl.pallas_call(
        kernel,
        in_specs=[pl.BlockSpec(memory_space=space) for space in spaces],
        out_specs=[pl.BlockSpec(memory_space=pl.ANY if x.hbm else pltpu.VMEM) for x in outs],
        out_shape=[(pltpu.HBM if x.hbm else pltpu.VMEM)(x.shape, x.dtype) for x in outs],
        scratch_shapes=list(scratch),
        input_output_aliases=aliases or {},
        compiler_params=pltpu.CompilerParams(vmem_limit_bytes=5 * 1024 * 1024),
        cost_estimate=pl.CostEstimate(flops=int(micros * FLOPS_PER_US), bytes_accessed=0, transcendentals=0),
        name=name,
    )(*scalars, *in_vmem(ins), *hbm)


class Out:
    def __init__(self, shape, dtype, hbm=False):
        self.shape, self.dtype, self.hbm = shape, dtype, hbm


def plan(cuts, held, width):
    out = []
    for m in range(held):
        lo = 0
        for units in cuts[0] if m < held - 1 else cuts[1]:
            out.append((m, lo, units * UNIT))
            lo += units * UNIT
        assert lo == width
    return out


class Ring:
    def __init__(self, n_row):
        self.n_row = n_row
        self.chips = n_row // 2
        self.half = self.chips // 2
        order = list(range(self.half)) + [self.chips + self.half - 1 - p for p in range(self.half, self.chips)]
        up, down, swap = [], [], []
        for pos in range(self.chips):
            for core in range(2):
                here = order[pos] * 2 + core
                step = 1 - 2 * core
                up.append((here, order[(pos + step) % self.chips] * 2 + core))
                down.append((here, order[(pos - step) % self.chips] * 2 + core))
                swap.append((here, order[pos] * 2 + 1 - core))
        self.up, self.down, self.swap = up, down, swap

    def onward(self, x):
        return lax.ppermute(x, "row", self.up)

    def backward(self, x):
        return lax.ppermute(x, "row", self.down)

    def partner(self, x):
        return lax.ppermute(x, "row", self.swap)

    def blocks(self, me):
        chip, core = lax.div(me, 2), lax.rem(me, 2)
        flip = self.chips + self.half - 1
        pos = jnp.where(chip < self.half, chip, flip - chip)

        def index(p, c):
            p = lax.rem(p + 2 * self.chips, self.chips)
            return jnp.where(p < self.half, p, flip - p) * 2 + c

        out = []
        for c, step in ((core, 1 - 2 * core), (1 - core, 2 * core - 1)):
            out.append(index(pos, c))
            for t in range(1, self.half):
                out.append(index(pos - step * t, c))
                out.append(index(pos - step * t, 1 - c))
            out.append(index(pos - step * self.half, c))
        return out


def slopes(pre):
    turn = jnp.tanh(0.5 * pre)
    sig = 0.5 * turn + 0.5
    rest = 1.0 - sig
    spread = sig * rest
    one = sig + pre * spread
    two = spread * (2.0 - pre * turn)
    return pre * sig, one, two


def inverse_norm(g):
    return 1.0 / jnp.sqrt(jnp.sum(g * g, axis=-1, keepdims=True) + EPS)


def strips(start, rows):
    return [pl.ds(start + r, STRIP) for r in range(0, rows, STRIP)]


def spans(cols):
    step = LANES if cols > LANES else cols // 2
    return [pl.ds(c, step) for c in range(0, cols, step)]


def cut_out(weight_a, places, info, *earlier):
    size = weight_a.shape[1]

    def kernel(*refs):
        weight_ref, sems = refs[1], refs[-1]
        copies = []
        for i, (m, lo, cols) in enumerate(places):
            out_ref = refs[2 + len(earlier) + i]
            copies.append(pltpu.make_async_copy(weight_ref.at[m, :, pl.ds(lo, cols)], out_ref, sems.at[i]))
            copies[-1].start()
        for copy in copies:
            copy.wait()

    return resident(
        kernel,
        "cut_out",
        [],
        [Out((size, cols), BF16) for _, _, cols in places],
        [info],
        [pltpu.SemaphoreType.DMA((len(places),))],
        [weight_a, *earlier],
    )


def permute_action(action, ring, info):
    rows, width = action.shape
    count = 2 * ring.chips
    size = width // count
    if size % 128:
        order = jnp.stack(ring.blocks(info[0]))
        moved = jnp.take(action.reshape(rows, count, size), order, axis=1).reshape(rows, width)
        return moved, moved.T

    def kernel(info_ref, x_ref, out_ref, turned_ref):
        for j, block in enumerate(ring.blocks(info_ref[0])):
            x = x_ref[:, pl.ds(pl.multiple_of(block * size, size), size)]
            out_ref[:, pl.ds(j * size, size)] = x
            turned_ref[pl.ds(j * size, size), :] = x.astype(F32).T.astype(BF16)

    return resident(
        kernel, "permute_action", [action], [Out((rows, width), BF16), Out((width, rows), BF16)], [info]
    )


def front(member, lo, action, state, pieces, value_w, carry):
    rows, width = action.shape
    size, cols = pieces[0].shape
    n_in = 3 + len(pieces)

    def kernel(*refs):
        action_ref, state_ref, value_ref = refs[:3]
        rest = refs[3:n_in]
        q_ref, g_ref, pre_ref, tangent_ref = refs[-4:]

        def weights(span):
            return jnp.concatenate([r[:, span] for r in rest], axis=0)

        for span in spans(cols):
            pre_ref[:, span] = jnp.dot(action_ref[...], weights(span), preferred_element_type=F32)
        for i, span in enumerate(spans(cols)):
            here = pl.ds(lo + span.start, span.size)
            value = value_ref[pl.ds(member, 1), here].astype(F32)
            for cut in strips(0, rows):
                pre = pre_ref[cut, span] + state_ref[member, cut, here].astype(F32)
                hidden, one, _ = slopes(pre)
                prod = hidden * value
                lanes = prod[:, :128]
                for c in range(128, span.size, 128):
                    lanes = lanes + prod[:, c : c + 128]
                if i:
                    lanes = lanes + q_ref[cut, :]
                elif carry is not None:
                    lanes = lanes + refs[n_in][cut, :]
                q_ref[cut, :] = lanes
                tangent_ref[cut, span] = (one * value).astype(BF16)
            g = lax.dot_general(
                tangent_ref[:, span], weights(span), (((1,), (1,)), ((), ())), preferred_element_type=F32
            )
            if i:
                g = g + g_ref[...]
            elif carry is not None:
                g = g + refs[n_in + 1][...]
            g_ref[...] = g

    ins = [action, state, value_w, *pieces, *(carry or [])]
    return resident(
        kernel,
        "front",
        ins,
        [Out((rows, 128), F32), Out((rows, width), F32)],
        scratch=[pltpu.VMEM((rows, cols), F32), pltpu.VMEM((rows, cols), BF16)],
        aliases={} if carry is None else {n_in: 0, n_in + 1: 1},
        micros=cols / 512,
    )


def unit_sums(info, grads):
    rows, width = grads[0].shape
    half = rows // 2
    part = half // 2

    def kernel(info_ref, *refs):
        bit = lax.rem(info_ref[1], 2)
        g_refs, outs, square_ref = refs[:-5], refs[-5:-1], refs[-1]
        for i, out_ref in enumerate(outs):
            side = bit if i < 2 else 1 - bit
            for r in range(0, part, STRIP):
                cut = pl.ds(pl.multiple_of(side * half + (i % 2) * part + r, STRIP), STRIP)
                total, square = None, None
                for g_ref in g_refs:
                    g = g_ref[cut, :]
                    unit = (g * inverse_norm(g)).astype(BF16).astype(F32)
                    length = jnp.sum(unit * unit, axis=-1, keepdims=True)
                    total = unit if total is None else total + unit
                    square = length if square is None else square + length
                square_ref[cut, :] = square
                out_ref[pl.ds(r, STRIP), :] = total.astype(out_ref.dtype)

    outs = [Out((part, width), F32)] * 2 + [Out((part, width), BF16)] * 2 + [Out((rows, 1), F32)]
    return resident(kernel, "unit_sums", grads, outs, [info])


def add_part(kept, got, scale, minus):
    def kernel(kept_ref, got_ref, *refs):
        total_ref, sent_ref = refs[-2:]
        for cut in strips(0, kept.shape[0]):
            total = kept_ref[cut, :] + got_ref[cut, :].astype(F32)
            total_ref[cut, :] = total
            if minus is not None:
                total = total - scale * refs[0][cut, :].astype(F32)
            sent_ref[cut, :] = total.astype(BF16)

    ins = [kept, got] + ([] if minus is None else [minus])
    return resident(kernel, "add_part", ins, [Out(kept.shape, F32), Out(kept.shape, BF16)])


def cotangent(info, members, n_member, kept, sent, got, turned_action, square, q, target, g):
    rows, width = g.shape
    half = rows // 2
    part = half // 2

    pairs = members * (members - 1)
    scale = 2.0 * ETA / pairs

    def kernel(info_ref, *refs):
        bit = lax.rem(info_ref[1], 2)
        counted = jnp.where(info_ref[1] < 2, 1.0, 0.0)
        kept_refs, sent_refs, got_refs, turned_action_ref = refs[:2], refs[2:4], refs[4:6], refs[6]
        square_ref, q_ref, target_ref, g_ref, cot_ref, left_ref, resid_ref, addend_ref, cot32_ref = refs[7:]
        resid_ref[...] = jnp.sum(q_ref[...], axis=-1, keepdims=True) - target_ref[...]
        left_ref[:, pl.ds(0, rows)] = turned_action_ref[...]
        for i in range(4):
            side = bit if i < 2 else 1 - bit
            for r in range(0, part, STRIP):
                here = pl.ds(r, STRIP)
                cut = pl.ds(pl.multiple_of(side * half + (i % 2) * part + r, STRIP), STRIP)
                if i < 2:
                    total = kept_refs[i][here, :]
                else:
                    total = n_member * sent_refs[i - 2][here, :].astype(F32) + got_refs[i - 2][here, :].astype(F32)
                grad = g_ref[cut, :]
                inverse = inverse_norm(grad)
                unit = grad * inverse
                direction = scale * (total - unit.astype(BF16).astype(F32))
                along = jnp.sum(unit * direction, axis=-1, keepdims=True)
                cot = (direction - unit * along) * inverse
                cot32_ref[cut, :] = cot
                cot_ref[cut, :] = cot.astype(BF16)
                addend = -square_ref[cut, :]
                if i < 2:
                    addend = addend + counted * jnp.sum(total * total, axis=-1, keepdims=True)
                addend_ref[cut, :] = addend * (1.0 / pairs)
        for r in range(0, rows, 128):
            left_ref[:, pl.ds(rows + r, 128)] = cot32_ref[pl.ds(r, 128), :].T.astype(BF16)

    return resident(
        kernel,
        "cotangent",
        [*kept, *sent, *got, turned_action, square, q, target, g],
        [Out((rows, width), BF16), Out((width, 2 * rows), BF16), Out((rows, 1), F32), Out((rows, 1), F32)],
        [info],
        [pltpu.VMEM((rows, width), F32)],
    )


def back(member, lo, cols, offset, action, state, cot, left, pieces, value_w, resid, grads):
    rows, width = cot.shape
    held = value_w.shape[0]
    n_in = 6 + len(pieces)
    mid = width // 2

    def kernel(*refs):
        action_ref, state_ref, cot_ref, left_ref, value_ref, resid_ref = refs[:6]
        rest = refs[6:n_in]
        grad_ref, sums_ref, top_ref, bottom_ref, pre_ref, back_ref, dpre_ref, tangent_ref, sems = refs[-9:]
        copies = []
        for span in spans(cols):
            inner = pl.ds(offset + span.start, span.size)
            weights = jnp.concatenate([r[:, inner] for r in rest], axis=0)
            pre_ref[:, span] = jnp.dot(action_ref[...], weights, preferred_element_type=F32)
            back_ref[:, span] = jnp.dot(cot_ref[...], weights, preferred_element_type=F32)
        for i, span in enumerate(spans(cols)):
            here = pl.ds(lo + span.start, span.size)
            value = value_ref[pl.ds(member, 1), here].astype(F32)
            sums = jnp.zeros((8, span.size), F32)
            for cut in strips(0, rows):
                hidden, one, two = slopes(pre_ref[cut, span] + state_ref[member, cut, here].astype(F32))
                back_term = back_ref[cut, span]
                resid_here = resid_ref[cut, :]
                dpre_ref[cut, span] = (value * (one * resid_here + two * back_term)).astype(BF16)
                tangent_ref[cut, span] = (one * value).astype(BF16)
                term = hidden * resid_here + one * back_term
                for s in range(0, STRIP, 8):
                    sums = sums + term[s : s + 8]
            sums_ref[member, :, here] = jnp.sum(sums, axis=0, keepdims=True)
            copies.append(pltpu.make_async_copy(dpre_ref.at[:, span], grad_ref.at[member, :, here], sems.at[i]))
            copies[-1].start()
            right = jnp.concatenate([dpre_ref[:, span], tangent_ref[:, span]], axis=0)
            bottom_ref[:, span] = jnp.dot(
                left_ref[pl.ds(mid, mid), :], right, preferred_element_type=F32
            ).astype(BF16)
            top_ref[:, span] = jnp.dot(left_ref[pl.ds(0, mid), :], right, preferred_element_type=F32).astype(BF16)
        for copy in copies:
            copy.wait()

    ins = [action, state, cot, left, value_w, resid, *pieces]
    hbm, aliases = [], {}
    if grads is not None:
        ins.append(grads[1])
        hbm.append(grads[0])
        aliases = {n_in: 1, n_in + 1: 0}
    return resident(
        kernel,
        "back",
        ins,
        [
            Out(state.shape, BF16, hbm=True),
            Out((held, 1, state.shape[-1]), F32),
            Out((mid, cols), BF16),
            Out((mid, cols), BF16),
        ],
        scratch=[
            pltpu.VMEM((rows, cols), F32),
            pltpu.VMEM((rows, cols), F32),
            pltpu.VMEM((rows, cols), BF16),
            pltpu.VMEM((rows, cols), BF16),
            pltpu.SemaphoreType.DMA((len(spans(cols)),)),
        ],
        hbm=hbm,
        aliases=aliases,
        micros=cols / 400,
    )


def combine(size, jobs, final, weight_grad, shape):
    ins, outs, scratch = [], [], []
    places = {}

    def take(addends):
        out = []
        for array, block in addends:
            if id(array) not in places:
                places[id(array)] = len(ins)
                ins.append(array)
            out.append((places[id(array)], block))
        return out

    sums = [[take(addends) for addends in job] for job in jobs]
    for job in jobs:
        outs.append(Out((len(job) * size, job[0][0][0].shape[1]), BF16))
    hbm, aliases = [], {}
    if final is not None:
        member, lo, addends = final
        cols = addends[0][0].shape[1]
        last = take(addends)
        outs.append(Out(shape, BF16, hbm=True))
        scratch = [pltpu.VMEM((size, cols), BF16), pltpu.SemaphoreType.DMA(())]
        if weight_grad is not None:
            hbm.append(weight_grad)
            aliases = {len(ins): len(jobs)}

    def kernel(*refs):
        results = refs[len(ins) + len(hbm) :]

        def add(addends, r):
            total = None
            for i, block in addends:
                x = refs[i][pl.ds(block * size + r, STRIP), :].astype(F32)
                total = x if total is None else total + x
            return total.astype(BF16)

        if final is not None:
            held_ref, sem = results[-2:]
            for r in range(0, size, STRIP):
                held_ref[pl.ds(r, STRIP), :] = add(last, r)
            copy = pltpu.make_async_copy(held_ref, results[len(jobs)].at[member, :, pl.ds(lo, cols)], sem)
            copy.start()
        for i, job in enumerate(sums):
            for p, addends in enumerate(job):
                for r in range(0, size, STRIP):
                    results[i][pl.ds(p * size + r, STRIP), :] = add(addends, r)
        if final is not None:
            copy.wait()

    got = resident(kernel, "combine", ins, outs, scratch=scratch, hbm=hbm, aliases=aliases)
    return got[: len(jobs)], (got[-1] if final is not None else weight_grad)


def exchange(x, axis, size, bit):
    def kernel(x_ref, y_ref, out_ref):
        out_ref[...] = x_ref[...] + y_ref[...]

    other = lax.ppermute(x, axis, [(i, i ^ bit) for i in range(size)])
    return resident(kernel, "add_two", [x, other], [Out(x.shape, x.dtype)])[0]


def member_total(kept, sent, size):
    pair = [(i, i ^ 1) for i in range(size)]
    firsts = [lax.ppermute(x, "member", pair) for x in sent]
    totals, got = list(kept), list(firsts)
    bit = 1
    while bit < size:
        bit *= 2
        swap = [(i, i ^ bit) for i in range(size)] if bit < size else pair
        for i in range(len(totals)):
            totals[i], x = add_part(totals[i], got[i], size, None if bit < size else firsts[i])
            got[i] = lax.ppermute(x, "member", swap)
    return totals, got


def body(n_member, n_row, action, state_term, target, weight_a, value_w):
    ring = Ring(n_row)
    chips, half = ring.chips, ring.half
    held, size, hidden_width = weight_a.shape
    members = held * n_member
    info = jnp.stack([lax.axis_index("row"), lax.axis_index("member")]).astype(jnp.int32)
    target_col = target[:, None]

    chunks = plan(GATHER_CUTS, held, hidden_width)
    count = len(chunks)
    owns = cut_out(weight_a, chunks[:1], info, target_col)
    owns += cut_out(weight_a, chunks[1:], info, owns[0])
    action_here, turned_action = permute_action(action, ring, info)
    pieces, carry = {}, [None] * held
    links, chains, swaps = [], {}, {}

    def send(x, *earlier):
        links.append(ring.onward(tie(x, *links[-3:-2], *earlier)))
        return links[-1]

    def run_front(c):
        m, lo, _ = chunks[c]
        carry[m] = front(m, lo, action_here, state_term, pieces[m, lo], value_w, carry[m])
        return carry[m][0]

    def open_chunk(c, *earlier):
        m, lo, cols = chunks[c]
        own = owns[c]
        first = ring.partner(own)
        mine, a, b = [], own, first
        for _ in range(1, half):
            a = send(a, *earlier)
            b = send(b)
            mine += [a, b]
        chains[c] = (a, mine, first)
        swaps[c] = [ring.partner(x) for x in mine]

    def close_chunk(c):
        m, lo, _ = chunks[c]
        a, mine, first = chains[c]
        last = send(a)
        pieces[m, lo] = [owns[c]] + mine + [last, first] + swaps[c] + [ring.partner(last)]

    open_chunk(0)
    for c in range(1, count):
        open_chunk(c, *([run_front(c - 3)] if c >= 3 else []))
        close_chunk(c - 1)
    close_chunk(count - 1)
    for c in range(max(count - 3, 0), count):
        run_front(c)
    gs = [c[1] for c in carry]

    *kept_sent, square = unit_sums(info, gs)
    kept, sent = kept_sent[:2], kept_sent[2:]
    totals, got = member_total(kept, sent, n_member)
    cots = [
        cotangent(info, members, n_member, totals, sent, got, turned_action, square, q, target_col, g)
        for q, g in carry
    ]
    diversity = cots[0][3]

    chunks = plan(SCATTER_CUTS, held, hidden_width)
    count = len(chunks)
    grads = weight_grad = None
    tops, others, flows, swapped = {}, {}, {}, {}
    queue = []

    def run_back(c, *earlier):
        nonlocal grads
        m, lo, cols = chunks[c]
        start = max(l for mm, l in pieces if mm == m and l <= lo)
        cot, left, resid, _ = cots[m]
        if earlier:
            resid = tie(resid, *earlier)
        *grads, tops[c], bottom = back(
            m, lo, cols, lo - start, action_here, state_term, cot, left, pieces[m, start],
            value_w, resid, grads,
        )
        others[c] = ring.partner(bottom)
        return bottom

    def addends(c, place, *more):
        return [(tops[c], place), (others[c], place), *more]

    lead = 3
    for c in range(lead - 1):
        run_back(c, *([x[0] for x in cots] if c else []))
    steps = count + 2 * half - 1
    finish_at = {}
    for c in range(count):
        finish_at.setdefault(min(c + 2 * half, steps - 1), []).append(c)
    after, value_grads = None, []
    stages, last_row = n_row.bit_length() - 1, count + 1 - lead
    for s in range(steps):
        jobs, labels = [], []
        if last_row <= s and len(value_grads) < stages + 1:
            value_grads.append(exchange(value_grads[-1], "row", n_row, 1 << (len(value_grads) - 1)))
            tops[s - 2] = tie(tops[s - 2], value_grads[-1])
        if s in (5, 6):
            diversity = exchange(diversity, "member", n_member, s - 4)
            tops[s] = tie(tops[s], diversity)
        if after is not None and s < count:
            tops[s] = tie(tops[s], after)
        for t in range(half):
            c = s - 2 * t
            if not 0 <= c < count:
                continue
            job = [addends(c, 2 * (half - t) - 1, *([(flows[c], 0)] if t else []))]
            if t:
                job.append(addends(c, 2 * (half - t), *([(flows[c], 1)] if t > 1 else [])))
            jobs.append(job)
            labels.append((c, t))
        finals = [
            (chunks[c][0], chunks[c][1], addends(c, 0, (flows[c], 0), (swapped[c], 1)))
            for c in finish_at.get(s, [])
        ]
        for final in finals[:-1]:
            _, weight_grad = combine(size, [], final, weight_grad, weight_a.shape)
        outs, weight_grad = combine(size, jobs, finals[-1] if finals else None, weight_grad, weight_a.shape)
        after = None
        if s == 0:
            run_back(lead - 1, outs[0])
        if s + lead < count:
            after = run_back(s + lead, outs[0])
            if s + lead == count - 1:
                value_grads = [grads[1]]
        for (c, t), x in zip(labels, outs):
            flows[c] = ring.backward(tie(x, *queue[-3:-2]))
            queue.append(flows[c])
            if t == half - 1:
                swapped[c] = ring.partner(flows[c])
    value_grad = value_grads[-1]
    while len(value_grads) < stages + 1:
        value_grad = exchange(value_grad, "row", n_row, 1 << (len(value_grads) - 1))
        value_grads.append(value_grad)
    bit = 4
    while bit < n_member:
        diversity = exchange(diversity, "member", n_member, bit)
        bit *= 2
    state_grad = grads[0]
    return weight_grad, value_grad[:, 0, :], state_grad, diversity[:, 0]


def solution(mesh):
    in_specs = (
        P("row", None),
        P("member", "row", None),
        P("row"),
        P("member", "row", None),
        P("member", None),
    )
    out_specs = (P("member", "row", None), P("member", None), P("member", "row", None), P("row"))
    step = functools.partial(body, mesh.shape["member"], mesh.shape["row"])
    return jax.shard_map(step, mesh=mesh, in_specs=in_specs, out_specs=out_specs, check_vma=False)
```

```python
import functools

import jax
import jax.numpy as jnp
from jax import lax
from jax.experimental import pallas as pl
from jax.experimental.pallas import tpu as pltpu
from jax.sharding import PartitionSpec as P

EPS = 1e-06
ETA = 5.0
UNIT = 512
GATHER_CUTS = ((4, 4), (4, 2, 1, 1))
SCATTER_CUTS = ((1, 1, 2, 2, 2), (2, 2, 2, 1, 1))
LANES = 512
STRIP = 16
F32 = jnp.float32
BF16 = jnp.bfloat16
FLOPS_PER_US = 1153500000


def tie(x, *earlier):
    return lax.optimization_barrier((x,) + earlier)[0]


def in_vmem(xs):
    return [pltpu.with_memory_space_constraint(x, pltpu.VMEM) for x in xs]


def resident(kernel, name, ins, outs, scalars=(), scratch=(), hbm=(), aliases=None, micros=0.7):
    spaces = [pltpu.SMEM] * len(scalars) + [pltpu.VMEM] * len(ins) + [pl.ANY] * len(hbm)
    return pl.pallas_call(
        kernel,
        in_specs=[pl.BlockSpec(memory_space=space) for space in spaces],
        out_specs=[pl.BlockSpec(memory_space=pl.ANY if x.hbm else pltpu.VMEM) for x in outs],
        out_shape=[(pltpu.HBM if x.hbm else pltpu.VMEM)(x.shape, x.dtype) for x in outs],
        scratch_shapes=list(scratch),
        input_output_aliases=aliases or {},
        compiler_params=pltpu.CompilerParams(vmem_limit_bytes=6 * 1024 * 1024),
        cost_estimate=pl.CostEstimate(flops=int(micros * FLOPS_PER_US), bytes_accessed=0, transcendentals=0),
        name=name,
    )(*scalars, *in_vmem(ins), *[pltpu.with_memory_space_constraint(x, pltpu.HBM) for x in hbm])


class Out:
    def __init__(self, shape, dtype, hbm=False):
        self.shape, self.dtype, self.hbm = shape, dtype, hbm


def plan(cuts, held, width):
    out = []
    for m in range(held):
        lo = 0
        for units in cuts[0] if m < held - 1 else cuts[1]:
            out.append((m, lo, units * UNIT))
            lo += units * UNIT
        assert lo == width
    return out


class Ring:
    def __init__(self, n_row):
        self.n_row = n_row
        self.chips = n_row // 2
        self.half = self.chips // 2
        order = list(range(self.half)) + [self.chips + self.half - 1 - p for p in range(self.half, self.chips)]
        up, down, swap = [], [], []
        for pos in range(self.chips):
            for core in range(2):
                here = order[pos] * 2 + core
                step = 1 - 2 * core
                up.append((here, order[(pos + step) % self.chips] * 2 + core))
                down.append((here, order[(pos - step) % self.chips] * 2 + core))
                swap.append((here, order[pos] * 2 + 1 - core))
        self.up, self.down, self.swap = up, down, swap

    def onward(self, x):
        return lax.ppermute(x, "row", self.up)

    def backward(self, x):
        return lax.ppermute(x, "row", self.down)

    def partner(self, x):
        return lax.ppermute(x, "row", self.swap)

    def blocks(self, me):
        chip, core = lax.div(me, 2), lax.rem(me, 2)
        flip = self.chips + self.half - 1
        pos = jnp.where(chip < self.half, chip, flip - chip)

        def index(p, c):
            p = lax.rem(p + 2 * self.chips, self.chips)
            return jnp.where(p < self.half, p, flip - p) * 2 + c

        out = []
        for c, step in ((core, 1 - 2 * core), (1 - core, 2 * core - 1)):
            out.append(index(pos, c))
            for t in range(1, self.half):
                out.append(index(pos - step * t, c))
                out.append(index(pos - step * t, 1 - c))
            out.append(index(pos - step * self.half, c))
        return out


def slopes(pre):
    turn = jnp.tanh(0.5 * pre)
    sig = 0.5 * turn + 0.5
    rest = 1.0 - sig
    spread = sig * rest
    one = sig + pre * spread
    two = spread * (2.0 - pre * turn)
    return pre * sig, one, two


def inverse_norm(g):
    return 1.0 / jnp.sqrt(jnp.sum(g * g, axis=-1, keepdims=True) + EPS)


def strips(start, rows):
    return [pl.ds(start + r, STRIP) for r in range(0, rows, STRIP)]


def each_strip(rows, work, start=None):
    step = 4 * STRIP if rows % (4 * STRIP) == 0 else STRIP

    def run(i, carry):
        for r in range(0, step, STRIP):
            carry = work(pl.ds(pl.multiple_of(i * step + r, STRIP), STRIP), carry)
        return carry

    return lax.fori_loop(0, rows // step, run, start)


def spans(cols):
    step = LANES if cols > LANES else cols // 2
    return [pl.ds(c, step) for c in range(0, cols, step)]


def cut_out(weight_a, places, info, *earlier):
    size = weight_a.shape[1]

    def kernel(*refs):
        weight_ref, sems = refs[1 + len(earlier)], refs[-1]
        copies = []
        for i, (m, lo, cols) in enumerate(places):
            out_ref = refs[2 + len(earlier) + i]
            copies.append(pltpu.make_async_copy(weight_ref.at[m, :, pl.ds(lo, cols)], out_ref, sems.at[i]))
            copies[-1].start()
        for copy in copies:
            copy.wait()

    return resident(
        kernel,
        "cut_out",
        list(earlier),
        [Out((size, cols), BF16) for _, _, cols in places],
        [info],
        [pltpu.SemaphoreType.DMA((len(places),))],
        [weight_a],
    )


def permute_action(action, ring, info):
    rows, width = action.shape
    count = 2 * ring.chips
    size = width // count
    if size % 128:
        order = jnp.stack(ring.blocks(info[0]))
        moved = jnp.take(action.reshape(rows, count, size), order, axis=1).reshape(rows, width)
        return moved, moved.T

    def kernel(info_ref, x_ref, out_ref, turned_ref):
        for j, block in enumerate(ring.blocks(info_ref[0])):
            x = x_ref[:, pl.ds(pl.multiple_of(block * size, size), size)]
            out_ref[:, pl.ds(j * size, size)] = x
            turned_ref[pl.ds(j * size, size), :] = x.astype(F32).T.astype(BF16)

    return resident(
        kernel, "permute_action", [action], [Out((rows, width), BF16), Out((width, rows), BF16)], [info]
    )


def front(member, lo, action, state, pieces, value_w, carry):
    rows, width = action.shape
    size, cols = pieces[0].shape
    n_in = 3 + len(pieces)

    def kernel(*refs):
        action_ref, state_ref, value_ref = refs[:3]
        rest = refs[3:n_in]
        q_ref, g_ref, pre_ref, tangent_ref = refs[-4:]

        def weights(span):
            return jnp.concatenate([r[:, span] for r in rest], axis=0)

        for span in spans(cols):
            pre_ref[:, span] = jnp.dot(action_ref[...], weights(span), preferred_element_type=F32)
        for i, span in enumerate(spans(cols)):
            here = pl.ds(lo + span.start, span.size)
            value = value_ref[pl.ds(member, 1), here].astype(F32)

            def work(cut, _):
                pre = pre_ref[cut, span] + state_ref[member, cut, here].astype(F32)
                hidden, one, _ = slopes(pre)
                prod = hidden * value
                lanes = prod[:, :128]
                for c in range(128, span.size, 128):
                    lanes = lanes + prod[:, c : c + 128]
                if i:
                    lanes = lanes + q_ref[cut, :]
                elif carry is not None:
                    lanes = lanes + refs[n_in][cut, :]
                q_ref[cut, :] = lanes
                tangent_ref[cut, span] = (one * value).astype(BF16)

            each_strip(rows, work)
            g = lax.dot_general(
                tangent_ref[:, span], weights(span), (((1,), (1,)), ((), ())), preferred_element_type=F32
            )
            if i:
                g = g + g_ref[...]
            elif carry is not None:
                g = g + refs[n_in + 1][...]
            g_ref[...] = g

    ins = [action, state, value_w, *pieces, *(carry or [])]
    return resident(
        kernel,
        "front",
        ins,
        [Out((rows, 128), F32), Out((rows, width), F32)],
        scratch=[pltpu.VMEM((rows, cols), F32), pltpu.VMEM((rows, cols), BF16)],
        aliases={} if carry is None else {n_in: 0, n_in + 1: 1},
        micros=cols / 512,
    )


def unit_sums(info, grads):
    rows, width = grads[0].shape
    half = rows // 2
    part = half // 2

    def kernel(info_ref, *refs):
        bit = lax.rem(info_ref[1], 2)
        g_refs, outs, square_ref = refs[:-5], refs[-5:-1], refs[-1]
        for i, out_ref in enumerate(outs):
            side = bit if i < 2 else 1 - bit
            base = side * half + (i % 2) * part

            def work(here, _):
                cut = pl.ds(pl.multiple_of(base + here.start, STRIP), STRIP)
                total, square = None, None
                for g_ref in g_refs:
                    g = g_ref[cut, :]
                    unit = (g * inverse_norm(g)).astype(BF16).astype(F32)
                    length = jnp.sum(unit * unit, axis=-1, keepdims=True)
                    total = unit if total is None else total + unit
                    square = length if square is None else square + length
                square_ref[cut, :] = square
                out_ref[here, :] = total.astype(out_ref.dtype)

            each_strip(part, work)

    outs = [Out((part, width), F32)] * 2 + [Out((part, width), BF16)] * 2 + [Out((rows, 1), F32)]
    return resident(kernel, "unit_sums", grads, outs, [info])


def add_part(kept, got, scale, minus):
    def kernel(kept_ref, got_ref, *refs):
        total_ref, sent_ref = refs[-2:]
        for cut in strips(0, kept.shape[0]):
            total = kept_ref[cut, :] + got_ref[cut, :].astype(F32)
            total_ref[cut, :] = total
            if minus is not None:
                total = total - scale * refs[0][cut, :].astype(F32)
            sent_ref[cut, :] = total.astype(BF16)

    ins = [kept, got] + ([] if minus is None else [minus])
    return resident(kernel, "add_part", ins, [Out(kept.shape, F32), Out(kept.shape, BF16)])


def cotangent(info, members, n_member, kept, sent, got, turned_action, square, q, target, g):
    rows, width = g.shape
    half = rows // 2
    part = half // 2

    pairs = members * (members - 1)
    scale = 2.0 * ETA / pairs

    def kernel(info_ref, *refs):
        bit = lax.rem(info_ref[1], 2)
        counted = jnp.where(info_ref[1] < 2, 1.0, 0.0)
        kept_refs, sent_refs, got_refs, turned_action_ref = refs[:2], refs[2:4], refs[4:6], refs[6]
        square_ref, q_ref, target_ref, g_ref, cot_ref, left_ref, resid_ref, addend_ref, cot32_ref = refs[7:]
        square_shape = (128, 128)
        diagonal = lax.broadcasted_iota(jnp.int32, square_shape, 0) == lax.broadcasted_iota(jnp.int32, square_shape, 1)
        for r in range(0, rows, 128):
            spread = jnp.broadcast_to(target_ref[:, pl.ds(r, 128)], square_shape)
            column = jnp.sum(jnp.where(diagonal, spread, 0.0), axis=-1, keepdims=True)
            cut = pl.ds(r, 128)
            resid_ref[cut, :] = jnp.sum(q_ref[cut, :], axis=-1, keepdims=True) - column
        left_ref[:, pl.ds(0, rows)] = turned_action_ref[...]
        for i in range(4):
            side = bit if i < 2 else 1 - bit
            base = side * half + (i % 2) * part

            def work(here, _):
                cut = pl.ds(pl.multiple_of(base + here.start, STRIP), STRIP)
                if i < 2:
                    total = kept_refs[i][here, :]
                else:
                    total = n_member * sent_refs[i - 2][here, :].astype(F32) + got_refs[i - 2][here, :].astype(F32)
                grad = g_ref[cut, :]
                inverse = inverse_norm(grad)
                unit = grad * inverse
                direction = scale * (total - unit.astype(BF16).astype(F32))
                along = jnp.sum(unit * direction, axis=-1, keepdims=True)
                cot = (direction - unit * along) * inverse
                cot32_ref[cut, :] = cot
                cot_ref[cut, :] = cot.astype(BF16)
                addend = -square_ref[cut, :]
                if i < 2:
                    addend = addend + counted * jnp.sum(total * total, axis=-1, keepdims=True)
                addend_ref[cut, :] = addend * (1.0 / pairs)

            each_strip(part, work)
        for r in range(0, rows, 128):
            left_ref[:, pl.ds(rows + r, 128)] = cot32_ref[pl.ds(r, 128), :].T.astype(BF16)

    return resident(
        kernel,
        "cotangent",
        [*kept, *sent, *got, turned_action, square, q, target, g],
        [Out((rows, width), BF16), Out((width, 2 * rows), BF16), Out((rows, 1), F32), Out((rows, 1), F32)],
        [info],
        [pltpu.VMEM((rows, width), F32)],
    )


def back(member, lo, cols, offset, action, state, cot, left, pieces, value_w, resid, grads):
    rows, width = cot.shape
    held = value_w.shape[0]
    n_in = 6 + len(pieces)
    mid = width // 2

    def kernel(*refs):
        action_ref, state_ref, cot_ref, left_ref, value_ref, resid_ref = refs[:6]
        rest = refs[6:n_in]
        grad_ref, sums_ref, top_ref, bottom_ref, pre_ref, back_ref, dpre_ref, tangent_ref, sems = refs[-9:]
        copies = []
        for span in spans(cols):
            inner = pl.ds(offset + span.start, span.size)
            weights = jnp.concatenate([r[:, inner] for r in rest], axis=0)
            pre_ref[:, span] = jnp.dot(action_ref[...], weights, preferred_element_type=F32)
            back_ref[:, span] = jnp.dot(cot_ref[...], weights, preferred_element_type=F32)
        for i, span in enumerate(spans(cols)):
            here = pl.ds(lo + span.start, span.size)
            value = value_ref[pl.ds(member, 1), here].astype(F32)

            def work(cut, sums):
                hidden, one, two = slopes(pre_ref[cut, span] + state_ref[member, cut, here].astype(F32))
                back_term = back_ref[cut, span]
                resid_here = resid_ref[cut, :]
                dpre_ref[cut, span] = (value * (one * resid_here + two * back_term)).astype(BF16)
                tangent_ref[cut, span] = (one * value).astype(BF16)
                term = hidden * resid_here + one * back_term
                for s in range(0, STRIP, 8):
                    sums = sums + term[s : s + 8]
                return sums

            sums = jnp.zeros((8, span.size), F32)
            for cut in strips(0, rows):
                sums = work(cut, sums)
            sums_ref[member, :, here] = jnp.sum(sums, axis=0, keepdims=True)
            copies.append(pltpu.make_async_copy(dpre_ref.at[:, span], grad_ref.at[member, :, here], sems.at[i]))
            copies[-1].start()
            right = jnp.concatenate([dpre_ref[:, span], tangent_ref[:, span]], axis=0)
            bottom_ref[:, span] = jnp.dot(
                left_ref[pl.ds(mid, mid), :], right, preferred_element_type=F32
            ).astype(BF16)
            top_ref[:, span] = jnp.dot(left_ref[pl.ds(0, mid), :], right, preferred_element_type=F32).astype(BF16)
        for copy in copies:
            copy.wait()

    ins = [action, state, cot, left, value_w, resid, *pieces]
    hbm, aliases = [], {}
    if grads is not None:
        ins.append(grads[1])
        hbm.append(grads[0])
        aliases = {n_in: 1, n_in + 1: 0}
    return resident(
        kernel,
        "back",
        ins,
        [
            Out(state.shape, BF16, hbm=True),
            Out((held, 1, state.shape[-1]), F32),
            Out((mid, cols), BF16),
            Out((mid, cols), BF16),
        ],
        scratch=[
            pltpu.VMEM((rows, cols), F32),
            pltpu.VMEM((rows, cols), F32),
            pltpu.VMEM((rows, cols), BF16),
            pltpu.VMEM((rows, cols), BF16),
            pltpu.SemaphoreType.DMA((len(spans(cols)),)),
        ],
        hbm=hbm,
        aliases=aliases,
        micros=cols / 200,
    )


def combine(size, jobs, final, weight_grad, shape):
    ins, outs, scratch = [], [], []
    places = {}

    def take(addends):
        out = []
        for array, block in addends:
            if id(array) not in places:
                places[id(array)] = len(ins)
                ins.append(array)
            out.append((places[id(array)], block))
        return out

    sums = [[take(addends) for addends in job] for job in jobs]
    for job in jobs:
        outs.append(Out((len(job) * size, job[0][0][0].shape[1]), BF16))
    hbm, aliases = [], {}
    if final is not None:
        member, lo, addends = final
        cols = addends[0][0].shape[1]
        last = take(addends)
        outs.append(Out(shape, BF16, hbm=True))
        scratch = [pltpu.VMEM((size, cols), BF16), pltpu.SemaphoreType.DMA(())]
        if weight_grad is not None:
            hbm.append(weight_grad)
            aliases = {len(ins): len(jobs)}

    def kernel(*refs):
        results = refs[len(ins) + len(hbm) :]

        def add(addends, to_ref, place):
            def work(cut, _):
                total = None
                for i, block in addends:
                    here = pl.ds(pl.multiple_of(block * size + cut.start, STRIP), STRIP)
                    x = refs[i][here, :].astype(F32)
                    total = x if total is None else total + x
                to_ref[pl.ds(pl.multiple_of(place * size + cut.start, STRIP), STRIP), :] = total.astype(BF16)

            each_strip(size, work)

        if final is not None:
            held_ref, sem = results[-2:]
            add(last, held_ref, 0)
            copy = pltpu.make_async_copy(held_ref, results[len(jobs)].at[member, :, pl.ds(lo, cols)], sem)
            copy.start()
        for i, job in enumerate(sums):
            for p, addends in enumerate(job):
                add(addends, results[i], p)
        if final is not None:
            copy.wait()

    got = resident(kernel, "combine", ins, outs, scratch=scratch, hbm=hbm, aliases=aliases)
    return got[: len(jobs)], (got[-1] if final is not None else weight_grad)


def all_sum(x, axis, size):
    others = [lax.ppermute(x, axis, [(i, i ^ k) for i in range(size)]) for k in range(1, size)]

    def kernel(*refs):
        values = [ref[...] for ref in refs[:-1]]
        while len(values) > 1:
            values = [values[i] + values[i + 1] for i in range(0, len(values), 2)]
        refs[-1][...] = values[0]

    return resident(kernel, "all_sum", [x, *others], [Out(x.shape, x.dtype)])[0]


def member_total(kept, sent, size):
    pair = [(i, i ^ 1) for i in range(size)]
    firsts = [lax.ppermute(x, "member", pair) for x in sent]
    totals, got = list(kept), list(firsts)
    bit = 1
    while bit < size:
        bit *= 2
        swap = [(i, i ^ bit) for i in range(size)] if bit < size else pair
        for i in range(len(totals)):
            totals[i], x = add_part(totals[i], got[i], size, None if bit < size else firsts[i])
            got[i] = lax.ppermute(x, "member", swap)
    return totals, got


def body(n_member, n_row, action, state_term, target, weight_a, value_w):
    ring = Ring(n_row)
    chips, half = ring.chips, ring.half
    held, size, hidden_width = weight_a.shape
    members = held * n_member
    info = jnp.stack([lax.axis_index("row"), lax.axis_index("member")]).astype(jnp.int32)
    target_row = target[None, :]

    chunks = plan(GATHER_CUTS, held, hidden_width)
    count = len(chunks)
    owns = cut_out(weight_a, chunks[:1], info)
    owns += cut_out(weight_a, chunks[1:], info, owns[0])
    action_here, turned_action = permute_action(action, ring, info)
    pieces, carry = {}, [None] * held
    links, chains, swaps = [], {}, {}

    def send(x, *earlier):
        links.append(ring.onward(tie(x, *links[-4:-3], *earlier)))
        return links[-1]

    def run_front(c):
        m, lo, _ = chunks[c]
        carry[m] = front(m, lo, action_here, state_term, pieces[m, lo], value_w, carry[m])
        return carry[m][0]

    def open_chunk(c, *earlier):
        m, lo, cols = chunks[c]
        own = owns[c]
        first = ring.partner(own)
        mine, a, b = [], own, first
        for _ in range(1, half):
            a = send(a, *earlier)
            b = send(b)
            mine += [a, b]
        chains[c] = (a, mine, first)
        swaps[c] = [ring.partner(x) for x in mine]

    def close_chunk(c):
        m, lo, _ = chunks[c]
        a, mine, first = chains[c]
        last = send(a)
        pieces[m, lo] = [owns[c]] + mine + [last, first] + swaps[c] + [ring.partner(last)]

    open_chunk(0)
    for c in range(1, count):
        open_chunk(c, *([run_front(c - 2)] if c >= 2 else []))
        close_chunk(c - 1)
    close_chunk(count - 1)
    for c in range(max(count - 2, 0), count):
        run_front(c)
    gs = [c[1] for c in carry]

    *kept_sent, square = unit_sums(info, gs)
    kept, sent = kept_sent[:2], kept_sent[2:]
    totals, got = member_total(kept, sent, n_member)
    cots = []

    def run_cotangent(m, *earlier):
        q, g = carry[m]
        if earlier:
            q = tie(q, *earlier)
        cots.append(
            cotangent(info, members, n_member, totals, sent, got, turned_action, square, q, target_row, g)
        )

    run_cotangent(0)

    chunks = plan(SCATTER_CUTS, held, hidden_width)
    count = len(chunks)
    grads = weight_grad = None
    tops, others, flows, swapped = {}, {}, {}, {}
    queue = []

    def run_back(c, *earlier):
        nonlocal grads
        m, lo, cols = chunks[c]
        start = max(l for mm, l in pieces if mm == m and l <= lo)
        cot, left, resid, _ = cots[m]
        if earlier:
            resid = tie(resid, *earlier)
        *grads, tops[c], bottom = back(
            m, lo, cols, lo - start, action_here, state_term, cot, left, pieces[m, start],
            value_w, resid, grads,
        )
        others[c] = ring.partner(bottom)
        return bottom

    def addends(c, place, *more):
        return [(tops[c], place), (others[c], place), *more]

    first = run_back(0)
    for m in range(1, held):
        run_cotangent(m, first)
    run_back(1, cots[-1][0])
    steps = count + 2 * half - 1
    finish_at, backs_at = {}, {}
    for c in range(count):
        finish_at.setdefault(min(c + 2 * half, steps - 1), []).append(c)
        if c > 1:
            backs_at.setdefault(max(c - 3, c // 2), []).append(c)
    after = None
    for s in range(steps):
        jobs, labels = [], []
        low = min(s - 2, count - 1)
        if s == count + 2:
            value_grad = all_sum(grads[1], "row", n_row)
            diversity = all_sum(cots[0][3], "member", n_member)
            tops[low] = tie(tops[low], value_grad, diversity)
        if s - 3 in swapped and s - 2 < count:
            tops[s - 2] = tie(tops[s - 2], swapped[s - 3])
        if after is not None and s < count:
            tops[s] = tie(tops[s], after)
        for t in range(half):
            c = s - 2 * t
            if not 0 <= c < count:
                continue
            job = [addends(c, 2 * (half - t) - 1, *([(flows[c], 0)] if t else []))]
            if t < half - 1:
                job.append(addends(c, 2 * (half - 1 - t), *([(flows[c], 1)] if t else [])))
            jobs.append(job)
            labels.append((c, t))
        finals = [
            (chunks[c][0], chunks[c][1], addends(c, 0, (flows[c], 0), (swapped[c], 1)))
            for c in finish_at.get(s, [])
        ]
        for final in finals[:-1]:
            _, weight_grad = combine(size, [], final, weight_grad, weight_a.shape)
        outs, weight_grad = combine(size, jobs, finals[-1] if finals else None, weight_grad, weight_a.shape)
        after = outs[0] if outs else None
        for (c, t), x in zip(labels, outs):
            flows[c] = ring.backward(tie(x, *queue[-3:-2]))
            queue.append(flows[c])
            if t == half - 2:
                swapped[c] = ring.partner(flows[c])
        for c in backs_at.get(s, []):
            early = {3: [0], 5: [1]}.get(c, [])
            after = run_back(c, outs[0], others[c - 2], *[flows[e] for e in early])
    state_grad = grads[0]
    value_grad, diversity = tie(value_grad, weight_grad), tie(diversity, weight_grad)
    return weight_grad, value_grad[:, 0, :], state_grad, diversity[:, 0]


def solution(mesh):
    in_specs = (
        P("row", None),
        P("member", "row", None),
        P("row"),
        P("member", "row", None),
        P("member", None),
    )
    out_specs = (P("member", "row", None), P("member", None), P("member", "row", None), P("row"))
    step = functools.partial(body, mesh.shape["member"], mesh.shape["row"])
    return jax.shard_map(step, mesh=mesh, in_specs=in_specs, out_specs=out_specs, check_vma=False)
```

```python
import functools

import jax
import jax.numpy as jnp
from jax import lax
from jax.experimental import pallas as pl
from jax.experimental.pallas import tpu as pltpu
from jax.sharding import PartitionSpec as P

EPS = 1e-06
ETA = 5.0
UNIT = 512
GATHER_CUTS = ((4, 4), (4, 2, 1, 1))
SCATTER_CUTS = ((1, 1, 2, 2, 2), (2, 2, 2, 1, 1))
LANES = 512
STRIP = 16
F32 = jnp.float32
BF16 = jnp.bfloat16
FLOPS_PER_US = 1153500000


def tie(x, *earlier):
    return lax.optimization_barrier((x,) + earlier)[0]


def in_vmem(xs):
    return [pltpu.with_memory_space_constraint(x, pltpu.VMEM) for x in xs]


def resident(kernel, name, ins, outs, scalars=(), scratch=(), hbm=(), aliases=None, micros=0.7):
    spaces = [pltpu.SMEM] * len(scalars) + [pltpu.VMEM] * len(ins) + [pl.ANY] * len(hbm)
    return pl.pallas_call(
        kernel,
        in_specs=[pl.BlockSpec(memory_space=space) for space in spaces],
        out_specs=[pl.BlockSpec(memory_space=pl.ANY if x.hbm else pltpu.VMEM) for x in outs],
        out_shape=[(pltpu.HBM if x.hbm else pltpu.VMEM)(x.shape, x.dtype) for x in outs],
        scratch_shapes=list(scratch),
        input_output_aliases=aliases or {},
        compiler_params=pltpu.CompilerParams(vmem_limit_bytes=6 * 1024 * 1024),
        cost_estimate=pl.CostEstimate(flops=int(micros * FLOPS_PER_US), bytes_accessed=0, transcendentals=0),
        name=name,
    )(*scalars, *in_vmem(ins), *[pltpu.with_memory_space_constraint(x, pltpu.HBM) for x in hbm])


class Out:
    def __init__(self, shape, dtype, hbm=False):
        self.shape, self.dtype, self.hbm = shape, dtype, hbm


def plan(cuts, held, width):
    out = []
    for m in range(held):
        lo = 0
        for units in cuts[0] if m < held - 1 else cuts[1]:
            out.append((m, lo, units * UNIT))
            lo += units * UNIT
        assert lo == width
    return out


class Ring:
    def __init__(self, n_row):
        self.n_row = n_row
        self.chips = n_row // 2
        self.half = self.chips // 2
        order = list(range(self.half)) + [self.chips + self.half - 1 - p for p in range(self.half, self.chips)]
        up, down, swap = [], [], []
        for pos in range(self.chips):
            for core in range(2):
                here = order[pos] * 2 + core
                step = 1 - 2 * core
                up.append((here, order[(pos + step) % self.chips] * 2 + core))
                down.append((here, order[(pos - step) % self.chips] * 2 + core))
                swap.append((here, order[pos] * 2 + 1 - core))
        self.up, self.down, self.swap = up, down, swap

    def onward(self, x):
        return lax.ppermute(x, "row", self.up)

    def backward(self, x):
        return lax.ppermute(x, "row", self.down)

    def partner(self, x):
        return lax.ppermute(x, "row", self.swap)

    def blocks(self, me):
        chip, core = lax.div(me, 2), lax.rem(me, 2)
        flip = self.chips + self.half - 1
        pos = jnp.where(chip < self.half, chip, flip - chip)

        def index(p, c):
            p = lax.rem(p + 2 * self.chips, self.chips)
            return jnp.where(p < self.half, p, flip - p) * 2 + c

        out = []
        for c, step in ((core, 1 - 2 * core), (1 - core, 2 * core - 1)):
            out.append(index(pos, c))
            for t in range(1, self.half):
                out.append(index(pos - step * t, c))
                out.append(index(pos - step * t, 1 - c))
            out.append(index(pos - step * self.half, c))
        return out


def slopes(pre):
    turn = jnp.tanh(0.5 * pre)
    sig = 0.5 * turn + 0.5
    rest = 1.0 - sig
    spread = sig * rest
    one = sig + pre * spread
    two = spread * (2.0 - pre * turn)
    return pre * sig, one, two


def inverse_norm(g):
    return 1.0 / jnp.sqrt(jnp.sum(g * g, axis=-1, keepdims=True) + EPS)


def strips(start, rows):
    return [pl.ds(start + r, STRIP) for r in range(0, rows, STRIP)]


def each_strip(rows, work, start=None):
    step = 4 * STRIP if rows % (4 * STRIP) == 0 else STRIP

    def run(i, carry):
        for r in range(0, step, STRIP):
            carry = work(pl.ds(pl.multiple_of(i * step + r, STRIP), STRIP), carry)
        return carry

    return lax.fori_loop(0, rows // step, run, start)


def spans(cols):
    step = LANES if cols > LANES else cols // 2
    return [pl.ds(c, step) for c in range(0, cols, step)]


def cut_out(weight_a, places, info, *earlier):
    size = weight_a.shape[1]

    def kernel(*refs):
        weight_ref, sems = refs[1 + len(earlier)], refs[-1]
        copies = []
        for i, (m, lo, cols) in enumerate(places):
            out_ref = refs[2 + len(earlier) + i]
            copies.append(pltpu.make_async_copy(weight_ref.at[m, :, pl.ds(lo, cols)], out_ref, sems.at[i]))
            copies[-1].start()
        for copy in copies:
            copy.wait()

    return resident(
        kernel,
        "cut_out",
        list(earlier),
        [Out((size, cols), BF16) for _, _, cols in places],
        [info],
        [pltpu.SemaphoreType.DMA((len(places),))],
        [weight_a],
    )


def permute_action(action, ring, info):
    rows, width = action.shape
    count = 2 * ring.chips
    size = width // count
    if size % 128:
        order = jnp.stack(ring.blocks(info[0]))
        moved = jnp.take(action.reshape(rows, count, size), order, axis=1).reshape(rows, width)
        return moved, moved.T

    def kernel(info_ref, x_ref, out_ref, turned_ref):
        for j, block in enumerate(ring.blocks(info_ref[0])):
            x = x_ref[:, pl.ds(pl.multiple_of(block * size, size), size)]
            out_ref[:, pl.ds(j * size, size)] = x
            turned_ref[pl.ds(j * size, size), :] = x.astype(F32).T.astype(BF16)

    return resident(
        kernel, "permute_action", [action], [Out((rows, width), BF16), Out((width, rows), BF16)], [info]
    )


def front(member, lo, action, state, pieces, value_w, carry):
    rows, width = action.shape
    size, cols = pieces[0].shape
    n_in = 3 + len(pieces)

    def kernel(*refs):
        action_ref, state_ref, value_ref = refs[:3]
        rest = refs[3:n_in]
        q_ref, g_ref, pre_ref, tangent_ref = refs[-4:]

        def weights(span):
            return jnp.concatenate([r[:, span] for r in rest], axis=0)

        for span in spans(cols):
            pre_ref[:, span] = jnp.dot(action_ref[...], weights(span), preferred_element_type=F32)
        for i, span in enumerate(spans(cols)):
            here = pl.ds(lo + span.start, span.size)
            value = value_ref[pl.ds(member, 1), here].astype(F32)

            def work(cut, _):
                pre = pre_ref[cut, span] + state_ref[member, cut, here].astype(F32)
                hidden, one, _ = slopes(pre)
                prod = hidden * value
                lanes = prod[:, :128]
                for c in range(128, span.size, 128):
                    lanes = lanes + prod[:, c : c + 128]
                if i:
                    lanes = lanes + q_ref[cut, :]
                elif carry is not None:
                    lanes = lanes + refs[n_in][cut, :]
                q_ref[cut, :] = lanes
                tangent_ref[cut, span] = (one * value).astype(BF16)

            each_strip(rows, work)
            g = lax.dot_general(
                tangent_ref[:, span], weights(span), (((1,), (1,)), ((), ())), preferred_element_type=F32
            )
            if i:
                g = g + g_ref[...]
            elif carry is not None:
                g = g + refs[n_in + 1][...]
            g_ref[...] = g

    ins = [action, state, value_w, *pieces, *(carry or [])]
    return resident(
        kernel,
        "front",
        ins,
        [Out((rows, 128), F32), Out((rows, width), F32)],
        scratch=[pltpu.VMEM((rows, cols), F32), pltpu.VMEM((rows, cols), BF16)],
        aliases={} if carry is None else {n_in: 0, n_in + 1: 1},
        micros=cols / 512,
    )


def unit_sums(info, grads):
    rows, width = grads[0].shape
    half = rows // 2
    part = half // 2

    def kernel(info_ref, *refs):
        bit = lax.rem(info_ref[1], 2)
        g_refs, outs, square_ref = refs[:-5], refs[-5:-1], refs[-1]
        for i, out_ref in enumerate(outs):
            side = bit if i < 2 else 1 - bit
            base = side * half + (i % 2) * part

            def work(here, _):
                cut = pl.ds(pl.multiple_of(base + here.start, STRIP), STRIP)
                total, square = None, None
                for g_ref in g_refs:
                    g = g_ref[cut, :]
                    unit = (g * inverse_norm(g)).astype(BF16).astype(F32)
                    length = jnp.sum(unit * unit, axis=-1, keepdims=True)
                    total = unit if total is None else total + unit
                    square = length if square is None else square + length
                square_ref[cut, :] = square
                out_ref[here, :] = total.astype(out_ref.dtype)

            each_strip(part, work)

    outs = [Out((part, width), F32)] * 2 + [Out((part, width), BF16)] * 2 + [Out((rows, 1), F32)]
    return resident(kernel, "unit_sums", grads, outs, [info])


def add_part(kept, got, scale, minus):
    def kernel(kept_ref, got_ref, *refs):
        total_ref, sent_ref = refs[-2:]
        for cut in strips(0, kept.shape[0]):
            total = kept_ref[cut, :] + got_ref[cut, :].astype(F32)
            total_ref[cut, :] = total
            if minus is not None:
                total = total - scale * refs[0][cut, :].astype(F32)
            sent_ref[cut, :] = total.astype(BF16)

    ins = [kept, got] + ([] if minus is None else [minus])
    return resident(kernel, "add_part", ins, [Out(kept.shape, F32), Out(kept.shape, BF16)])


def cotangent(info, members, n_member, kept, sent, got, turned_action, square, q, target, g):
    rows, width = g.shape
    half = rows // 2
    part = half // 2

    pairs = members * (members - 1)
    scale = 2.0 * ETA / pairs

    def kernel(info_ref, *refs):
        bit = lax.rem(info_ref[1], 2)
        counted = jnp.where(info_ref[1] < 2, 1.0, 0.0)
        kept_refs, sent_refs, got_refs, turned_action_ref = refs[:2], refs[2:4], refs[4:6], refs[6]
        square_ref, q_ref, target_ref, g_ref, cot_ref, left_ref, resid_ref, addend_ref, cot32_ref = refs[7:]
        square_shape = (128, 128)
        diagonal = lax.broadcasted_iota(jnp.int32, square_shape, 0) == lax.broadcasted_iota(jnp.int32, square_shape, 1)
        for r in range(0, rows, 128):
            spread = jnp.broadcast_to(target_ref[:, pl.ds(r, 128)], square_shape)
            column = jnp.sum(jnp.where(diagonal, spread, 0.0), axis=-1, keepdims=True)
            cut = pl.ds(r, 128)
            resid_ref[cut, :] = jnp.sum(q_ref[cut, :], axis=-1, keepdims=True) - column
        left_ref[:, pl.ds(0, rows)] = turned_action_ref[...]
        for i in range(4):
            side = bit if i < 2 else 1 - bit
            base = side * half + (i % 2) * part

            def work(here, _):
                cut = pl.ds(pl.multiple_of(base + here.start, STRIP), STRIP)
                if i < 2:
                    total = kept_refs[i][here, :]
                else:
                    total = n_member * sent_refs[i - 2][here, :].astype(F32) + got_refs[i - 2][here, :].astype(F32)
                grad = g_ref[cut, :]
                inverse = inverse_norm(grad)
                unit = grad * inverse
                direction = scale * (total - unit.astype(BF16).astype(F32))
                along = jnp.sum(unit * direction, axis=-1, keepdims=True)
                cot = (direction - unit * along) * inverse
                cot32_ref[cut, :] = cot
                cot_ref[cut, :] = cot.astype(BF16)
                addend = -square_ref[cut, :]
                if i < 2:
                    addend = addend + counted * jnp.sum(total * total, axis=-1, keepdims=True)
                addend_ref[cut, :] = addend * (1.0 / pairs)

            each_strip(part, work)
        for r in range(0, rows, 128):
            left_ref[:, pl.ds(rows + r, 128)] = cot32_ref[pl.ds(r, 128), :].T.astype(BF16)

    return resident(
        kernel,
        "cotangent",
        [*kept, *sent, *got, turned_action, square, q, target, g],
        [Out((rows, width), BF16), Out((width, 2 * rows), BF16), Out((rows, 1), F32), Out((rows, 1), F32)],
        [info],
        [pltpu.VMEM((rows, width), F32)],
    )


def back(member, lo, cols, offset, action, state, cot, left, pieces, value_w, resid, grads):
    rows, width = cot.shape
    held = value_w.shape[0]
    n_in = 6 + len(pieces)
    mid = width // 2

    def kernel(*refs):
        action_ref, state_ref, cot_ref, left_ref, value_ref, resid_ref = refs[:6]
        rest = refs[6:n_in]
        grad_ref, sums_ref, top_ref, bottom_ref, pre_ref, back_ref, dpre_ref, tangent_ref, sems = refs[-9:]
        copies = []
        for span in spans(cols):
            inner = pl.ds(offset + span.start, span.size)
            weights = jnp.concatenate([r[:, inner] for r in rest], axis=0)
            pre_ref[:, span] = jnp.dot(action_ref[...], weights, preferred_element_type=F32)
            back_ref[:, span] = jnp.dot(cot_ref[...], weights, preferred_element_type=F32)
        for i, span in enumerate(spans(cols)):
            here = pl.ds(lo + span.start, span.size)
            value = value_ref[pl.ds(member, 1), here].astype(F32)

            def work(cut, sums):
                hidden, one, two = slopes(pre_ref[cut, span] + state_ref[member, cut, here].astype(F32))
                back_term = back_ref[cut, span]
                resid_here = resid_ref[cut, :]
                dpre_ref[cut, span] = (value * (one * resid_here + two * back_term)).astype(BF16)
                tangent_ref[cut, span] = (one * value).astype(BF16)
                term = hidden * resid_here + one * back_term
                for s in range(0, STRIP, 8):
                    sums = sums + term[s : s + 8]
                return sums

            sums = jnp.zeros((8, span.size), F32)
            for cut in strips(0, rows):
                sums = work(cut, sums)
            sums_ref[member, :, here] = jnp.sum(sums, axis=0, keepdims=True)
            copies.append(pltpu.make_async_copy(dpre_ref.at[:, span], grad_ref.at[member, :, here], sems.at[i]))
            copies[-1].start()
            right = jnp.concatenate([dpre_ref[:, span], tangent_ref[:, span]], axis=0)
            bottom_ref[:, span] = jnp.dot(
                left_ref[pl.ds(mid, mid), :], right, preferred_element_type=F32
            ).astype(BF16)
            top_ref[:, span] = jnp.dot(left_ref[pl.ds(0, mid), :], right, preferred_element_type=F32).astype(BF16)
        for copy in copies:
            copy.wait()

    ins = [action, state, cot, left, value_w, resid, *pieces]
    hbm, aliases = [], {}
    if grads is not None:
        ins.append(grads[1])
        hbm.append(grads[0])
        aliases = {n_in: 1, n_in + 1: 0}
    return resident(
        kernel,
        "back",
        ins,
        [
            Out(state.shape, BF16, hbm=True),
            Out((held, 1, state.shape[-1]), F32),
            Out((mid, cols), BF16),
            Out((mid, cols), BF16),
        ],
        scratch=[
            pltpu.VMEM((rows, cols), F32),
            pltpu.VMEM((rows, cols), F32),
            pltpu.VMEM((rows, cols), BF16),
            pltpu.VMEM((rows, cols), BF16),
            pltpu.SemaphoreType.DMA((len(spans(cols)),)),
        ],
        hbm=hbm,
        aliases=aliases,
        micros=cols / 200,
    )


def combine(size, jobs, final, weight_grad, shape):
    ins, outs, scratch = [], [], []
    places = {}

    def take(addends):
        out = []
        for array, block in addends:
            if id(array) not in places:
                places[id(array)] = len(ins)
                ins.append(array)
            out.append((places[id(array)], block))
        return out

    sums = [[take(addends) for addends in job] for job in jobs]
    for job in jobs:
        outs.append(Out((len(job) * size, job[0][0][0].shape[1]), BF16))
    hbm, aliases = [], {}
    if final is not None:
        member, lo, addends = final
        cols = addends[0][0].shape[1]
        last = take(addends)
        outs.append(Out(shape, BF16, hbm=True))
        scratch = [pltpu.VMEM((size, cols), BF16), pltpu.SemaphoreType.DMA(())]
        if weight_grad is not None:
            hbm.append(weight_grad)
            aliases = {len(ins): len(jobs)}

    def kernel(*refs):
        results = refs[len(ins) + len(hbm) :]

        def add(addends, to_ref, place):
            def work(cut, _):
                total = None
                for i, block in addends:
                    here = pl.ds(pl.multiple_of(block * size + cut.start, STRIP), STRIP)
                    x = refs[i][here, :].astype(F32)
                    total = x if total is None else total + x
                to_ref[pl.ds(pl.multiple_of(place * size + cut.start, STRIP), STRIP), :] = total.astype(BF16)

            each_strip(size, work)

        if final is not None:
            held_ref, sem = results[-2:]
            add(last, held_ref, 0)
            copy = pltpu.make_async_copy(held_ref, results[len(jobs)].at[member, :, pl.ds(lo, cols)], sem)
            copy.start()
        for i, job in enumerate(sums):
            for p, addends in enumerate(job):
                add(addends, results[i], p)
        if final is not None:
            copy.wait()

    got = resident(kernel, "combine", ins, outs, scratch=scratch, hbm=hbm, aliases=aliases)
    return got[: len(jobs)], (got[-1] if final is not None else weight_grad)


def all_sum(x, axis, size):
    others = [lax.ppermute(x, axis, [(i, i ^ k) for i in range(size)]) for k in range(1, size)]

    def kernel(*refs):
        values = [ref[...] for ref in refs[:-1]]
        while len(values) > 1:
            values = [values[i] + values[i + 1] for i in range(0, len(values), 2)]
        refs[-1][...] = values[0]

    return resident(kernel, "all_sum", [x, *others], [Out(x.shape, x.dtype)])[0]


def member_total(kept, sent, size):
    pair = [(i, i ^ 1) for i in range(size)]
    firsts = [lax.ppermute(x, "member", pair) for x in sent]
    totals, got = list(kept), list(firsts)
    bit = 1
    while bit < size:
        bit *= 2
        swap = [(i, i ^ bit) for i in range(size)] if bit < size else pair
        for i in range(len(totals)):
            totals[i], x = add_part(totals[i], got[i], size, None if bit < size else firsts[i])
            got[i] = lax.ppermute(x, "member", swap)
    return totals, got


def body(n_member, n_row, action, state_term, target, weight_a, value_w):
    ring = Ring(n_row)
    chips, half = ring.chips, ring.half
    held, size, hidden_width = weight_a.shape
    members = held * n_member
    info = jnp.stack([lax.axis_index("row"), lax.axis_index("member")]).astype(jnp.int32)
    target_row = target[None, :]

    chunks = plan(GATHER_CUTS, held, hidden_width)
    count = len(chunks)
    owns = cut_out(weight_a, chunks[:1], info)
    owns += cut_out(weight_a, chunks[1:], info, owns[0])
    action_here, turned_action = permute_action(action, ring, info)
    pieces, carry = {}, [None] * held
    links, chains, swaps = [], {}, {}

    def send(x, *earlier):
        links.append(ring.onward(tie(x, *links[-4:-3], *earlier)))
        return links[-1]

    def run_front(c):
        m, lo, _ = chunks[c]
        carry[m] = front(m, lo, action_here, state_term, pieces[m, lo], value_w, carry[m])
        return carry[m][0]

    def open_chunk(c, *earlier):
        m, lo, cols = chunks[c]
        own = owns[c]
        first = ring.partner(own)
        mine, a, b = [], own, first
        for _ in range(1, half):
            a = send(a, *earlier)
            b = send(b)
            mine += [a, b]
        chains[c] = (a, mine, first)
        swaps[c] = [ring.partner(x) for x in mine]

    def close_chunk(c):
        m, lo, _ = chunks[c]
        a, mine, first = chains[c]
        last = send(a)
        pieces[m, lo] = [owns[c]] + mine + [last, first] + swaps[c] + [ring.partner(last)]

    open_chunk(0)
    for c in range(1, count):
        open_chunk(c, *([run_front(c - 2)] if c >= 2 else []))
        close_chunk(c - 1)
    close_chunk(count - 1)
    for c in range(max(count - 2, 0), count):
        run_front(c)
    gs = [c[1] for c in carry]

    *kept_sent, square = unit_sums(info, gs)
    kept, sent = kept_sent[:2], kept_sent[2:]
    totals, got = member_total(kept, sent, n_member)
    cots = []

    def run_cotangent(m, *earlier):
        q, g = carry[m]
        if earlier:
            q = tie(q, *earlier)
        cots.append(
            cotangent(info, members, n_member, totals, sent, got, turned_action, square, q, target_row, g)
        )

    run_cotangent(0)

    chunks = plan(SCATTER_CUTS, held, hidden_width)
    count = len(chunks)
    grads = weight_grad = None
    tops, others, flows, swapped = {}, {}, {}, {}
    queue = []

    def run_back(c, *earlier):
        nonlocal grads
        m, lo, cols = chunks[c]
        start = max(l for mm, l in pieces if mm == m and l <= lo)
        cot, left, resid, _ = cots[m]
        if earlier:
            resid = tie(resid, *earlier)
        *grads, tops[c], bottom = back(
            m, lo, cols, lo - start, action_here, state_term, cot, left, pieces[m, start],
            value_w, resid, grads,
        )
        others[c] = ring.partner(bottom)
        return bottom

    def addends(c, place, *more):
        return [(tops[c], place), (others[c], place), *more]

    first = run_back(0)
    for m in range(1, held):
        run_cotangent(m, first)
    run_back(1, cots[-1][0])
    steps = count + 2 * half - 1
    finish_at, backs_at = {}, {}
    for c in range(count):
        finish_at.setdefault(min(c + 2 * half, steps - 1), []).append(c)
        if c > 1:
            backs_at.setdefault(max(c - 3, c // 2), []).append(c)
    after = None
    for s in range(steps):
        jobs, labels = [], []
        low = min(s - 2, count - 1)
        if s == count + 2:
            value_grad = all_sum(grads[1], "row", n_row)
            tops[low] = tie(tops[low], value_grad)
        if s - 3 in swapped and s - 2 < count:
            tops[s - 2] = tie(tops[s - 2], swapped[s - 3])
        if after is not None and s < count:
            tops[s] = tie(tops[s], after)
        for t in range(half):
            c = s - 2 * t
            if not 0 <= c < count:
                continue
            job = [addends(c, 2 * (half - t) - 1, *([(flows[c], 0)] if t else []))]
            if t < half - 1:
                job.append(addends(c, 2 * (half - 1 - t), *([(flows[c], 1)] if t else [])))
            jobs.append(job)
            labels.append((c, t))
        finals = [
            (chunks[c][0], chunks[c][1], addends(c, 0, (flows[c], 0), (swapped[c], 1)))
            for c in finish_at.get(s, [])
        ]
        for final in finals[:-1]:
            _, weight_grad = combine(size, [], final, weight_grad, weight_a.shape)
        outs, weight_grad = combine(size, jobs, finals[-1] if finals else None, weight_grad, weight_a.shape)
        after = outs[0] if outs else None
        for (c, t), x in zip(labels, outs):
            flows[c] = ring.backward(tie(x, *queue[-3:-2]))
            queue.append(flows[c])
            if t == half - 2:
                swapped[c] = ring.partner(flows[c])
        for c in backs_at.get(s, []):
            early = {3: [0], 5: [1]}.get(c, [])
            after = run_back(c, outs[0], others[c - 2], *[flows[e] for e in early])
    state_grad = grads[0]
    diversity = all_sum(tie(cots[0][3], flows[count - 1]), "member", n_member)
    value_grad, diversity = tie(value_grad, weight_grad), tie(diversity, weight_grad)
    return weight_grad, value_grad[:, 0, :], state_grad, diversity[:, 0]


def solution(mesh):
    in_specs = (
        P("row", None),
        P("member", "row", None),
        P("row"),
        P("member", "row", None),
        P("member", None),
    )
    out_specs = (P("member", "row", None), P("member", None), P("member", "row", None), P("row"))
    step = functools.partial(body, mesh.shape["member"], mesh.shape["row"])
    return jax.shard_map(step, mesh=mesh, in_specs=in_specs, out_specs=out_specs, check_vma=False)
```

```python
import functools

import jax
import jax.numpy as jnp
from jax import lax
from jax.experimental import pallas as pl
from jax.experimental.pallas import tpu as pltpu
from jax.sharding import PartitionSpec as P

EPS = 1e-06
ETA = 5.0
UNIT = 512
GATHER_CUTS = ((4, 4), (4, 2, 1, 1))
SCATTER_CUTS = ((1, 1, 2, 2, 2), (2, 2, 2, 1, 1))
LANES = 512
STRIP = 16
F32 = jnp.float32
BF16 = jnp.bfloat16
FLOPS_PER_US = 1153500000


def tie(x, *earlier):
    return lax.optimization_barrier((x,) + earlier)[0]


def in_vmem(xs):
    return [pltpu.with_memory_space_constraint(x, pltpu.VMEM) for x in xs]


def resident(kernel, name, ins, outs, scalars=(), scratch=(), hbm=(), aliases=None, micros=0.7):
    spaces = [pltpu.SMEM] * len(scalars) + [pltpu.VMEM] * len(ins) + [pl.ANY] * len(hbm)
    return pl.pallas_call(
        kernel,
        in_specs=[pl.BlockSpec(memory_space=space) for space in spaces],
        out_specs=[pl.BlockSpec(memory_space=pl.ANY if x.hbm else pltpu.VMEM) for x in outs],
        out_shape=[(pltpu.HBM if x.hbm else pltpu.VMEM)(x.shape, x.dtype) for x in outs],
        scratch_shapes=list(scratch),
        input_output_aliases=aliases or {},
        compiler_params=pltpu.CompilerParams(vmem_limit_bytes=6 * 1024 * 1024),
        cost_estimate=pl.CostEstimate(flops=int(micros * FLOPS_PER_US), bytes_accessed=0, transcendentals=0),
        name=name,
    )(*scalars, *in_vmem(ins), *[pltpu.with_memory_space_constraint(x, pltpu.HBM) for x in hbm])


class Out:
    def __init__(self, shape, dtype, hbm=False):
        self.shape, self.dtype, self.hbm = shape, dtype, hbm


def plan(cuts, held, width):
    out = []
    for m in range(held):
        lo = 0
        for units in cuts[0] if m < held - 1 else cuts[1]:
            out.append((m, lo, units * UNIT))
            lo += units * UNIT
        assert lo == width
    return out


class Ring:
    def __init__(self, n_row):
        self.n_row = n_row
        self.chips = n_row // 2
        self.half = self.chips // 2
        order = list(range(self.half)) + [self.chips + self.half - 1 - p for p in range(self.half, self.chips)]
        up, down, swap = [], [], []
        for pos in range(self.chips):
            for core in range(2):
                here = order[pos] * 2 + core
                step = 1 - 2 * core
                up.append((here, order[(pos + step) % self.chips] * 2 + core))
                down.append((here, order[(pos - step) % self.chips] * 2 + core))
                swap.append((here, order[pos] * 2 + 1 - core))
        self.up, self.down, self.swap = up, down, swap

    def onward(self, x):
        return lax.ppermute(x, "row", self.up)

    def backward(self, x):
        return lax.ppermute(x, "row", self.down)

    def partner(self, x):
        return lax.ppermute(x, "row", self.swap)

    def blocks(self, me):
        chip, core = lax.div(me, 2), lax.rem(me, 2)
        flip = self.chips + self.half - 1
        pos = jnp.where(chip < self.half, chip, flip - chip)

        def index(p, c):
            p = lax.rem(p + 2 * self.chips, self.chips)
            return jnp.where(p < self.half, p, flip - p) * 2 + c

        out = []
        for c, step in ((core, 1 - 2 * core), (1 - core, 2 * core - 1)):
            out.append(index(pos, c))
            for t in range(1, self.half):
                out.append(index(pos - step * t, c))
                out.append(index(pos - step * t, 1 - c))
            out.append(index(pos - step * self.half, c))
        return out


def slopes(pre):
    turn = jnp.tanh(0.5 * pre)
    sig = 0.5 * turn + 0.5
    rest = 1.0 - sig
    spread = sig * rest
    one = sig + pre * spread
    two = spread * (2.0 - pre * turn)
    return pre * sig, one, two


def inverse_norm(g):
    return 1.0 / jnp.sqrt(jnp.sum(g * g, axis=-1, keepdims=True) + EPS)


def strips(start, rows):
    return [pl.ds(start + r, STRIP) for r in range(0, rows, STRIP)]


def each_strip(rows, work, start=None):
    step = 4 * STRIP if rows % (4 * STRIP) == 0 else STRIP

    def run(i, carry):
        for r in range(0, step, STRIP):
            carry = work(pl.ds(pl.multiple_of(i * step + r, STRIP), STRIP), carry)
        return carry

    return lax.fori_loop(0, rows // step, run, start)


def spans(cols):
    step = LANES if cols > LANES else cols // 2
    return [pl.ds(c, step) for c in range(0, cols, step)]


def cut_out(weight_a, places, info, *earlier):
    size = weight_a.shape[1]

    def kernel(*refs):
        weight_ref, sems = refs[1 + len(earlier)], refs[-1]
        copies = []
        for i, (m, lo, cols) in enumerate(places):
            out_ref = refs[2 + len(earlier) + i]
            copies.append(pltpu.make_async_copy(weight_ref.at[m, :, pl.ds(lo, cols)], out_ref, sems.at[i]))
            copies[-1].start()
        for copy in copies:
            copy.wait()

    return resident(
        kernel,
        "cut_out",
        list(earlier),
        [Out((size, cols), BF16) for _, _, cols in places],
        [info],
        [pltpu.SemaphoreType.DMA((len(places),))],
        [weight_a],
    )


def permute_action(action, ring, info):
    rows, width = action.shape
    count = 2 * ring.chips
    size = width // count
    if size % 128:
        order = jnp.stack(ring.blocks(info[0]))
        moved = jnp.take(action.reshape(rows, count, size), order, axis=1).reshape(rows, width)
        return moved, moved.T

    def kernel(info_ref, x_ref, out_ref, turned_ref):
        for j, block in enumerate(ring.blocks(info_ref[0])):
            x = x_ref[:, pl.ds(pl.multiple_of(block * size, size), size)]
            out_ref[:, pl.ds(j * size, size)] = x
            turned_ref[pl.ds(j * size, size), :] = x.astype(F32).T.astype(BF16)

    return resident(
        kernel, "permute_action", [action], [Out((rows, width), BF16), Out((width, rows), BF16)], [info]
    )


def front(member, lo, action, state, pieces, value_w, carry):
    rows, width = action.shape
    size, cols = pieces[0].shape
    n_in = 3 + len(pieces)

    def kernel(*refs):
        action_ref, state_ref, value_ref = refs[:3]
        rest = refs[3:n_in]
        q_ref, g_ref, pre_ref, tangent_ref = refs[-4:]

        def weights(span):
            return jnp.concatenate([r[:, span] for r in rest], axis=0)

        for span in spans(cols):
            pre_ref[:, span] = jnp.dot(action_ref[...], weights(span), preferred_element_type=F32)
        for i, span in enumerate(spans(cols)):
            here = pl.ds(lo + span.start, span.size)
            value = value_ref[pl.ds(member, 1), here].astype(F32)

            def work(cut, _):
                pre = pre_ref[cut, span] + state_ref[member, cut, here].astype(F32)
                hidden, one, _ = slopes(pre)
                prod = hidden * value
                lanes = prod[:, :128]
                for c in range(128, span.size, 128):
                    lanes = lanes + prod[:, c : c + 128]
                if i:
                    lanes = lanes + q_ref[cut, :]
                elif carry is not None:
                    lanes = lanes + refs[n_in][cut, :]
                q_ref[cut, :] = lanes
                tangent_ref[cut, span] = (one * value).astype(BF16)

            each_strip(rows, work)
            g = lax.dot_general(
                tangent_ref[:, span], weights(span), (((1,), (1,)), ((), ())), preferred_element_type=F32
            )
            if i:
                g = g + g_ref[...]
            elif carry is not None:
                g = g + refs[n_in + 1][...]
            g_ref[...] = g

    ins = [action, state, value_w, *pieces, *(carry or [])]
    return resident(
        kernel,
        "front",
        ins,
        [Out((rows, 128), F32), Out((rows, width), F32)],
        scratch=[pltpu.VMEM((rows, cols), F32), pltpu.VMEM((rows, cols), BF16)],
        aliases={} if carry is None else {n_in: 0, n_in + 1: 1},
        micros=cols / 512,
    )


def unit_sums(info, grads):
    rows, width = grads[0].shape
    half = rows // 2
    part = half // 2

    def kernel(info_ref, *refs):
        bit = lax.rem(info_ref[1], 2)
        g_refs, outs, square_ref = refs[:-5], refs[-5:-1], refs[-1]
        for i, out_ref in enumerate(outs):
            side = bit if i < 2 else 1 - bit
            base = side * half + (i % 2) * part

            def work(here, _):
                cut = pl.ds(pl.multiple_of(base + here.start, STRIP), STRIP)
                total, square = None, None
                for g_ref in g_refs:
                    g = g_ref[cut, :]
                    unit = (g * inverse_norm(g)).astype(BF16).astype(F32)
                    length = jnp.sum(unit * unit, axis=-1, keepdims=True)
                    total = unit if total is None else total + unit
                    square = length if square is None else square + length
                square_ref[cut, :] = square
                out_ref[here, :] = total.astype(out_ref.dtype)

            each_strip(part, work)

    outs = [Out((part, width), F32)] * 2 + [Out((part, width), BF16)] * 2 + [Out((rows, 1), F32)]
    return resident(kernel, "unit_sums", grads, outs, [info])


def add_part(kept, got, scale, minus):
    def kernel(kept_ref, got_ref, *refs):
        total_ref, sent_ref, length_ref = refs[-3:]
        for cut in strips(0, kept.shape[0]):
            total = kept_ref[cut, :].astype(F32) + got_ref[cut, :].astype(F32)
            total_ref[cut, :] = total
            length_ref[cut, :] = jnp.sum(total * total, axis=-1, keepdims=True)
            if minus is not None:
                total = total - scale * refs[0][cut, :].astype(F32)
            sent_ref[cut, :] = total.astype(BF16)

    ins = [kept, got] + ([] if minus is None else [minus])
    rows = kept.shape[0]
    return resident(kernel, "add_part", ins, [Out(kept.shape, F32), Out(kept.shape, BF16), Out((rows, 1), F32)])


def cotangent(info, members, n_member, kept, sent, got, lengths, turned_action, square, q, target, g):
    rows, width = g.shape
    half = rows // 2
    part = half // 2

    pairs = members * (members - 1)
    scale = 2.0 * ETA / pairs

    def kernel(info_ref, *refs):
        bit = lax.rem(info_ref[1], 2)
        kept_refs, sent_refs, got_refs, length_refs = refs[:2], refs[2:4], refs[4:6], refs[6:10]
        turned_action_ref, square_ref, q_ref, target_ref, g_ref = refs[10:15]
        cot_ref, left_ref, resid_ref, diversity_ref, cot32_ref = refs[15:]
        square_shape = (128, 128)
        diagonal = lax.broadcasted_iota(jnp.int32, square_shape, 0) == lax.broadcasted_iota(jnp.int32, square_shape, 1)
        for r in range(0, rows, 128):
            spread = jnp.broadcast_to(target_ref[:, pl.ds(r, 128)], square_shape)
            column = jnp.sum(jnp.where(diagonal, spread, 0.0), axis=-1, keepdims=True)
            cut = pl.ds(r, 128)
            resid_ref[cut, :] = jnp.sum(q_ref[cut, :], axis=-1, keepdims=True) - column
        left_ref[:, pl.ds(0, rows)] = turned_action_ref[...]
        for i in range(4):
            side = bit if i < 2 else 1 - bit
            base = side * half + (i % 2) * part

            def work(here, _):
                cut = pl.ds(pl.multiple_of(base + here.start, STRIP), STRIP)
                if i < 2:
                    total = kept_refs[i][here, :]
                else:
                    total = n_member * sent_refs[i - 2][here, :].astype(F32) + got_refs[i - 2][here, :].astype(F32)
                grad = g_ref[cut, :]
                inverse = inverse_norm(grad)
                unit = grad * inverse
                direction = scale * (total - unit.astype(BF16).astype(F32))
                along = jnp.sum(unit * direction, axis=-1, keepdims=True)
                cot = (direction - unit * along) * inverse
                cot32_ref[cut, :] = cot
                cot_ref[cut, :] = cot.astype(BF16)
                diversity_ref[cut, :] = (length_refs[i][here, :] - square_ref[cut, :]) * (1.0 / pairs)

            each_strip(part, work)
        for r in range(0, rows, 128):
            left_ref[:, pl.ds(rows + r, 128)] = cot32_ref[pl.ds(r, 128), :].T.astype(BF16)

    return resident(
        kernel,
        "cotangent",
        [*kept, *sent, *got, *lengths, turned_action, square, q, target, g],
        [Out((rows, width), BF16), Out((width, 2 * rows), BF16), Out((rows, 1), F32), Out((rows, 1), F32)],
        [info],
        [pltpu.VMEM((rows, width), F32)],
    )


def back(member, lo, cols, offset, action, state, cot, left, pieces, value_w, resid, grads):
    rows, width = cot.shape
    held = value_w.shape[0]
    n_in = 6 + len(pieces)
    mid = width // 2

    def kernel(*refs):
        action_ref, state_ref, cot_ref, left_ref, value_ref, resid_ref = refs[:6]
        rest = refs[6:n_in]
        grad_ref, sums_ref, top_ref, bottom_ref, pre_ref, back_ref, dpre_ref, tangent_ref, sems = refs[-9:]
        copies = []
        for span in spans(cols):
            inner = pl.ds(offset + span.start, span.size)
            weights = jnp.concatenate([r[:, inner] for r in rest], axis=0)
            pre_ref[:, span] = jnp.dot(action_ref[...], weights, preferred_element_type=F32)
            back_ref[:, span] = jnp.dot(cot_ref[...], weights, preferred_element_type=F32)
        for i, span in enumerate(spans(cols)):
            here = pl.ds(lo + span.start, span.size)
            value = value_ref[pl.ds(member, 1), here].astype(F32)

            def work(cut, sums):
                hidden, one, two = slopes(pre_ref[cut, span] + state_ref[member, cut, here].astype(F32))
                back_term = back_ref[cut, span]
                resid_here = resid_ref[cut, :]
                dpre_ref[cut, span] = (value * (one * resid_here + two * back_term)).astype(BF16)
                tangent_ref[cut, span] = (one * value).astype(BF16)
                term = hidden * resid_here + one * back_term
                for s in range(0, STRIP, 8):
                    sums = sums + term[s : s + 8]
                return sums

            sums = jnp.zeros((8, span.size), F32)
            for cut in strips(0, rows):
                sums = work(cut, sums)
            sums_ref[member, :, here] = jnp.sum(sums, axis=0, keepdims=True)
            copies.append(pltpu.make_async_copy(dpre_ref.at[:, span], grad_ref.at[member, :, here], sems.at[i]))
            copies[-1].start()
            right = jnp.concatenate([dpre_ref[:, span], tangent_ref[:, span]], axis=0)
            bottom_ref[:, span] = jnp.dot(
                left_ref[pl.ds(mid, mid), :], right, preferred_element_type=F32
            ).astype(BF16)
            top_ref[:, span] = jnp.dot(left_ref[pl.ds(0, mid), :], right, preferred_element_type=F32).astype(BF16)
        for copy in copies:
            copy.wait()

    ins = [action, state, cot, left, value_w, resid, *pieces]
    hbm, aliases = [], {}
    if grads is not None:
        ins.append(grads[1])
        hbm.append(grads[0])
        aliases = {n_in: 1, n_in + 1: 0}
    return resident(
        kernel,
        "back",
        ins,
        [
            Out(state.shape, BF16, hbm=True),
            Out((held, 1, state.shape[-1]), F32),
            Out((mid, cols), BF16),
            Out((mid, cols), BF16),
        ],
        scratch=[
            pltpu.VMEM((rows, cols), F32),
            pltpu.VMEM((rows, cols), F32),
            pltpu.VMEM((rows, cols), BF16),
            pltpu.VMEM((rows, cols), BF16),
            pltpu.SemaphoreType.DMA((len(spans(cols)),)),
        ],
        hbm=hbm,
        aliases=aliases,
        micros=cols / 200,
    )


def combine(size, jobs, final, weight_grad, shape):
    ins, outs, scratch = [], [], []
    places = {}

    def take(addends):
        out = []
        for array, block in addends:
            if id(array) not in places:
                places[id(array)] = len(ins)
                ins.append(array)
            out.append((places[id(array)], block))
        return out

    sums = [[take(addends) for addends in job] for job in jobs]
    for job in jobs:
        outs.append(Out((len(job) * size, job[0][0][0].shape[1]), BF16))
    hbm, aliases = [], {}
    if final is not None:
        member, lo, addends = final
        cols = addends[0][0].shape[1]
        last = take(addends)
        outs.append(Out(shape, BF16, hbm=True))
        scratch = [pltpu.VMEM((size, cols), BF16), pltpu.SemaphoreType.DMA(())]
        if weight_grad is not None:
            hbm.append(weight_grad)
            aliases = {len(ins): len(jobs)}

    def kernel(*refs):
        results = refs[len(ins) + len(hbm) :]

        def add(addends, to_ref, place):
            def work(cut, _):
                total = None
                for i, block in addends:
                    here = pl.ds(pl.multiple_of(block * size + cut.start, STRIP), STRIP)
                    x = refs[i][here, :].astype(F32)
                    total = x if total is None else total + x
                to_ref[pl.ds(pl.multiple_of(place * size + cut.start, STRIP), STRIP), :] = total.astype(BF16)

            each_strip(size, work)

        if final is not None:
            held_ref, sem = results[-2:]
            add(last, held_ref, 0)
            copy = pltpu.make_async_copy(held_ref, results[len(jobs)].at[member, :, pl.ds(lo, cols)], sem)
            copy.start()
        for i, job in enumerate(sums):
            for p, addends in enumerate(job):
                add(addends, results[i], p)
        if final is not None:
            copy.wait()

    got = resident(kernel, "combine", ins, outs, scratch=scratch, hbm=hbm, aliases=aliases)
    return got[: len(jobs)], (got[-1] if final is not None else weight_grad)


def all_sum(x, axis, size):
    others = [lax.ppermute(x, axis, [(i, i ^ k) for i in range(size)]) for k in range(1, size)]

    def kernel(*refs):
        values = [ref[...] for ref in refs[:-1]]
        while len(values) > 1:
            values = [values[i] + values[i + 1] for i in range(0, len(values), 2)]
        refs[-1][...] = values[0]

    return resident(kernel, "all_sum", [x, *others], [Out(x.shape, x.dtype)])[0]


def add_two(x, y):
    def kernel(x_ref, y_ref, out_ref):
        out_ref[...] = x_ref[...] + y_ref[...]

    return resident(kernel, "add_two", [x, y], [Out(x.shape, x.dtype)])[0]


def member_total(kept, sent, square, size):
    pair = [(i, i ^ 1) for i in range(size)]
    firsts = [lax.ppermute(x, "member", pair) for x in sent]
    square = add_two(square, lax.ppermute(square, "member", pair))
    totals, got, lengths = list(kept), list(firsts), [None] * len(firsts)
    bit = 1
    while bit < size:
        bit *= 2
        swap = [(i, i ^ bit) for i in range(size)] if bit < size else pair
        for i in range(len(totals)):
            totals[i], x, lengths[i] = add_part(totals[i], got[i], size, None if bit < size else firsts[i])
            if i == len(totals) - 1:
                x = tie(x, square)
            got[i] = lax.ppermute(x, "member", swap)
            if bit < size:
                totals[i] = x
        if bit < size:
            square = add_two(square, lax.ppermute(square, "member", swap))
    return totals, got, lengths, [lax.ppermute(x, "member", pair) for x in lengths], square


def body(n_member, n_row, action, state_term, target, weight_a, value_w):
    ring = Ring(n_row)
    chips, half = ring.chips, ring.half
    held, size, hidden_width = weight_a.shape
    members = held * n_member
    info = jnp.stack([lax.axis_index("row"), lax.axis_index("member")]).astype(jnp.int32)
    target_row = target[None, :]

    chunks = plan(GATHER_CUTS, held, hidden_width)
    count = len(chunks)
    owns = cut_out(weight_a, chunks[:1], info)
    owns += cut_out(weight_a, chunks[1:], info, owns[0])
    action_here, turned_action = permute_action(action, ring, info)
    pieces, carry = {}, [None] * held
    links, chains, swaps = [], {}, {}

    def send(x, *earlier):
        links.append(ring.onward(tie(x, *links[-5:-4], *earlier)))
        return links[-1]

    def run_front(c):
        m, lo, _ = chunks[c]
        carry[m] = front(m, lo, action_here, state_term, pieces[m, lo], value_w, carry[m])
        return carry[m][0]

    def open_chunk(c, *earlier):
        m, lo, cols = chunks[c]
        own = owns[c]
        first = ring.partner(own)
        mine, a, b = [], own, first
        for _ in range(1, half):
            a = send(a, *earlier)
            b = send(b)
            mine += [a, b]
        chains[c] = (a, mine, first)
        swaps[c] = [ring.partner(x) for x in mine]

    def close_chunk(c):
        m, lo, _ = chunks[c]
        a, mine, first = chains[c]
        last = send(a)
        pieces[m, lo] = [owns[c]] + mine + [last, first] + swaps[c] + [ring.partner(last)]

    open_chunk(0)
    for c in range(1, count):
        open_chunk(c, *([run_front(c - 2)] if c >= 2 else []))
        close_chunk(c - 1)
    close_chunk(count - 1)
    for c in range(max(count - 2, 0), count):
        run_front(c)
    gs = [c[1] for c in carry]

    *kept_sent, square = unit_sums(info, gs)
    kept, sent = kept_sent[:2], kept_sent[2:]
    totals, got, lengths, got_lengths, square = member_total(kept, sent, square, n_member)
    cots = []

    def run_cotangent(m, *earlier):
        q, g = carry[m]
        if earlier:
            q = tie(q, *earlier)
        cots.append(
            cotangent(info, members, n_member, totals, sent, got, lengths + got_lengths, turned_action, square, q, target_row, g)
        )

    run_cotangent(0)

    chunks = plan(SCATTER_CUTS, held, hidden_width)
    count = len(chunks)
    grads = weight_grad = None
    tops, others, flows, swapped = {}, {}, {}, {}
    queue = []

    def run_back(c, *earlier):
        nonlocal grads
        m, lo, cols = chunks[c]
        start = max(l for mm, l in pieces if mm == m and l <= lo)
        cot, left, resid, _ = cots[m]
        if earlier:
            resid = tie(resid, *earlier)
        *grads, tops[c], bottom = back(
            m, lo, cols, lo - start, action_here, state_term, cot, left, pieces[m, start],
            value_w, resid, grads,
        )
        others[c] = ring.partner(bottom)
        return bottom

    def addends(c, place, *more):
        return [(tops[c], place), (others[c], place), *more]

    first = run_back(0)
    for m in range(1, held):
        run_cotangent(m, first)
    run_back(1, cots[-1][0])
    steps = count + 2 * half - 1
    finish_at, backs_at = {}, {}
    for c in range(count):
        finish_at.setdefault(min(c + 2 * half, steps - 1), []).append(c)
        if c > 1:
            backs_at.setdefault(max(c - 3, c // 2), []).append(c)
    after = None
    for s in range(steps):
        jobs, labels = [], []
        low = min(s - 2, count - 1)
        if s == count + 2:
            value_grad = all_sum(grads[1], "row", n_row)
            tops[low] = tie(tops[low], value_grad)
        if s - 3 in swapped and s - 2 < count:
            tops[s - 2] = tie(tops[s - 2], swapped[s - 3])
        if after is not None and s < count:
            tops[s] = tie(tops[s], after)
        for t in range(half):
            c = s - 2 * t
            if not 0 <= c < count:
                continue
            job = [addends(c, 2 * (half - t) - 1, *([(flows[c], 0)] if t else []))]
            if t < half - 1:
                job.append(addends(c, 2 * (half - 1 - t), *([(flows[c], 1)] if t else [])))
            jobs.append(job)
            labels.append((c, t))
        finals = [
            (chunks[c][0], chunks[c][1], addends(c, 0, (flows[c], 0), (swapped[c], 1)))
            for c in finish_at.get(s, [])
        ]
        for final in finals[:-1]:
            _, weight_grad = combine(size, [], final, weight_grad, weight_a.shape)
        outs, weight_grad = combine(size, jobs, finals[-1] if finals else None, weight_grad, weight_a.shape)
        after = outs[0] if outs else None
        for (c, t), x in zip(labels, outs):
            flows[c] = ring.backward(tie(x, *queue[-3:-2]))
            queue.append(flows[c])
            if t == half - 2:
                swapped[c] = ring.partner(flows[c])
        for c in backs_at.get(s, []):
            early = {3: [0], 5: [1]}.get(c, [])
            after = run_back(c, outs[0], others[c - 2], *[flows[e] for e in early])
    state_grad = grads[0]
    diversity = cots[0][3]
    value_grad, diversity = tie(value_grad, weight_grad), tie(diversity, weight_grad)
    return weight_grad, value_grad[:, 0, :], state_grad, diversity[:, 0]


def solution(mesh):
    in_specs = (
        P("row", None),
        P("member", "row", None),
        P("row"),
        P("member", "row", None),
        P("member", None),
    )
    out_specs = (P("member", "row", None), P("member", None), P("member", "row", None), P("row"))
    step = functools.partial(body, mesh.shape["member"], mesh.shape["row"])
    return jax.shard_map(step, mesh=mesh, in_specs=in_specs, out_specs=out_specs, check_vma=False)
```
